256 devices in a mesh: tm: 32 (over y, x, core), height: 8 (over z).
Axes of the slice: x: 4, y: 4, z: 8, core: 2. Of those that a mesh axis runs over, the one named last changes fastest.
Arguments:
- inputs: bfloat16 [64, 32, 64, 128], P('tm', 'height'), may hold values from -20 to 20
- gain_first: float32 [128], replicated, may hold values from 0.1 to 1.9
- shift_first: float32 [128], replicated, may hold values from -2 to 2
- weight_first: bfloat16 [3, 3, 3, 128, 128], replicated, may hold values from -0.109375 to 0.109375
- gain_second: float32 [128], replicated, may hold values from 0.1 to 1.9
- shift_second: float32 [128], replicated, may hold values from -2 to 2
- weight_second: bfloat16 [3, 3, 3, 128, 128], replicated, may hold values from -0.109375 to 0.109375
- upstream: bfloat16 [64, 32, 64, 128], P('tm', 'height'), may hold values from -12 to 12
Outputs:
- output: bfloat16 [64, 32, 64, 128], P('tm', 'height')
- input_grad: bfloat16 [64, 32, 64, 128], P('tm', 'height')
- weight_first_grad: float32 [3, 3, 3, 128, 128], replicated
- weight_second_grad: float32 [3, 3, 3, 128, 128], replicated
- gain_first_grad: float32 [128], replicated
- shift_first_grad: float32 [128], replicated
- gain_second_grad: float32 [128], replicated
- shift_second_grad: float32 [128], replicated
The draws below stay inside these ranges and needn't reach their ends.
All inputs are finite; a program needn't handle non-finite values.
Results may differ from the reference program's by a relative error of at most 0.012.
Values may be sent and summed in bfloat16 or wider, within the bound.
A program may use at most 64 MiB of HBM per device.

```python
import jax
import jax.numpy as jnp
from jax import lax

C = 128
G = 32
COLS = 64
FRAMES = 64
ROWS = 32


def ragged_factor(key, count, lowest):
    position = jnp.arange(count)
    factor = jnp.exp(jax.random.uniform(key, (count,), jnp.float32, jnp.log(lowest), 0.0))
    return jnp.where((position == 0) | (position == count - 1), 1.0, factor)


def rising_scale(key, frames_total, rows_total):
    time_key, row_key = jax.random.split(key, 2)
    time_pos = jnp.arange(frames_total, dtype=jnp.float32) / max(frames_total - 1, 1)
    row_pos = jnp.arange(rows_total, dtype=jnp.float32) / max(rows_total - 1, 1)
    time_part = 3.0 ** time_pos * ragged_factor(time_key, frames_total, 0.5)
    row_part = 1.5 ** row_pos * ragged_factor(row_key, rows_total, 0.6)
    return time_part[:, None, None, None] * row_part[None, :, None, None]


def draw_inputs(key, part):
    key = jax.random.fold_in(key, 11)
    noise_key = jax.random.fold_in(key, 0)
    centre_key = jax.random.fold_in(key, 1)
    scale_key = jax.random.fold_in(key, 3)
    level_key = jax.random.fold_in(key, 4)
    shape = (FRAMES, ROWS, COLS, C)
    scaling = rising_scale(scale_key, FRAMES, ROWS)
    frame_key, row_key = jax.random.split(level_key, 2)
    level = 0.4 * jax.random.uniform(frame_key, (FRAMES, 1, 1, 1), jnp.float32) * jax.random.uniform(row_key, (1, ROWS, 1, 1), jnp.float32)
    centres = jax.random.uniform(centre_key, (C,), jnp.float32, -0.5, 0.5)
    noise = jnp.clip(jax.random.normal(noise_key, shape, jnp.float32), -4.0, 4.0)
    return (noise * scaling + centres + level).astype(jnp.bfloat16)


def draw_upstream(key, part):
    key = jax.random.fold_in(key, 23)
    noise_key = jax.random.fold_in(key, 0)
    scale_key = jax.random.fold_in(key, 2)
    shape = (FRAMES, ROWS, COLS, C)
    scaling = 0.5 * rising_scale(scale_key, FRAMES, ROWS)
    values = jnp.clip(jax.random.normal(noise_key, shape, jnp.float32), -4.0, 4.0) * scaling
    return values.astype(jnp.bfloat16)


def normal_values(key, extent, scale, bound, kind=jnp.bfloat16):
    array = scale * jax.random.normal(key, extent, jnp.float32)
    return jnp.clip(array, min=-bound, max=bound).astype(kind)


def setup_inputs(seed: int = 0) -> dict:
    arg_keys = jax.random.split(jax.random.key(seed), 9)
    inputs = draw_inputs(jax.random.fold_in(arg_keys[8], 71), 0)
    gain_first = jnp.clip(1.0 + 0.18 * jax.random.normal(arg_keys[1], (C,), jnp.float32), 0.1, 1.9)
    shift_first = normal_values(arg_keys[2], (C,), 0.5, 2.0, jnp.float32)
    weight_first = normal_values(arg_keys[3], (3, 3, 3, C, C), (27 * C) ** -0.5, 0.109375)
    gain_second = jnp.clip(1.0 + 0.18 * jax.random.normal(arg_keys[4], (C,), jnp.float32), 0.1, 1.9)
    shift_second = normal_values(arg_keys[5], (C,), 0.5, 2.0, jnp.float32)
    weight_second = normal_values(arg_keys[6], (3, 3, 3, C, C), (27 * C) ** -0.5, 0.109375)
    upstream = draw_upstream(jax.random.fold_in(arg_keys[8], 71), 0)
    return dict(inputs=inputs, gain_first=gain_first, shift_first=shift_first, weight_first=weight_first, gain_second=gain_second, shift_second=shift_second, weight_second=weight_second, upstream=upstream)


epsilon = 1e-06

def rounded(values):
    return lax.optimization_barrier(values.astype(jnp.bfloat16))

def group_stats(values):
    shaped = values.reshape(values.shape[:3] + (G, C // G))
    centre = lax.optimization_barrier(jnp.mean(shaped, axis=(0, 1, 2, 4)))
    spread = lax.optimization_barrier(jnp.mean((shaped - centre[:, None]) ** 2, axis=(0, 1, 2, 4)))
    return (jnp.repeat(centre, C // G), jnp.repeat(lax.rsqrt(spread + epsilon), C // G))

def activate(values, centre, inverse, gain, offset):
    return jax.nn.silu((values - centre) * inverse * gain + offset)

def causal_conv(activated, weight):
    first_frame = activated[:1]
    extended = jnp.concatenate([first_frame, first_frame, activated], axis=0)
    extended = jnp.pad(extended, ((0, 0), (1, 1), (1, 1), (0, 0)))
    return lax.conv_general_dilated(extended[None], weight, (1, 1, 1), 'VALID', dimension_numbers=('NDHWC', 'DHWIO', 'NDHWC'), precision=lax.Precision.HIGHEST)[0]

def norm_back(act_grad, values, centre, inverse, gain, offset):
    normed = (values - centre) * inverse
    affine = normed * gain + offset
    sigmoid_val = jax.nn.sigmoid(affine)
    pre_grad = act_grad * sigmoid_val * (1.0 + affine * (1.0 - sigmoid_val))
    gain_grad = lax.optimization_barrier(jnp.sum(pre_grad * normed, axis=(0, 1, 2)))
    offset_grad = lax.optimization_barrier(jnp.sum(pre_grad, axis=(0, 1, 2)))
    members = float(values.shape[0] * values.shape[1] * values.shape[2] * (C // G))
    mean_grad = jnp.repeat((gain * offset_grad).reshape(G, -1).sum(axis=1) / members, C // G)
    mean_cross = jnp.repeat((gain * gain_grad).reshape(G, -1).sum(axis=1) / members, C // G)
    value_grad = inverse * (pre_grad * gain - mean_grad - normed * mean_cross)
    return (value_grad, gain_grad, offset_grad)

def reference(inputs, gain_first, shift_first, weight_first, gain_second, shift_second, weight_second, upstream):
    local_vals = inputs.astype(jnp.float32)
    centre_one, inverse_one = group_stats(local_vals)
    act_one = rounded(activate(local_vals, centre_one, inverse_one, gain_first, shift_first)).astype(jnp.float32)
    weight_one = weight_first.astype(jnp.float32)
    hidden_raw, conv_back_one = jax.vjp(causal_conv, act_one, weight_one)
    hidden_vals = rounded(hidden_raw).astype(jnp.float32)
    centre_two, inverse_two = group_stats(hidden_vals)
    act_two = rounded(activate(hidden_vals, centre_two, inverse_two, gain_second, shift_second)).astype(jnp.float32)
    weight_two = weight_second.astype(jnp.float32)
    branch, conv_back_two = jax.vjp(causal_conv, act_two, weight_two)
    output = (local_vals + branch).astype(jnp.bfloat16)
    grad_vals = upstream.astype(jnp.float32)
    act_grad_two, weight_second_grad = conv_back_two(grad_vals)
    value_two, gain_second_grad, shift_second_grad = norm_back(act_grad_two, hidden_vals, centre_two, inverse_two, gain_second, shift_second)
    hidden_grad = rounded(value_two).astype(jnp.float32)
    act_grad_one, weight_first_grad = conv_back_one(hidden_grad)
    value_one, gain_first_grad, shift_first_grad = norm_back(act_grad_one, local_vals, centre_one, inverse_one, gain_first, shift_first)
    input_grad = (grad_vals + value_one).astype(jnp.bfloat16)
    return (output, input_grad, weight_first_grad, weight_second_grad, gain_first_grad, shift_first_grad, gain_second_grad, shift_second_grad)
```

```python
import functools
import types

import jax
import jax.numpy as jnp
from jax import lax
from jax.experimental import pallas as pl
from jax.experimental.pallas import tpu as pltpu
from jax.sharding import PartitionSpec as P

C = 128
G = 32
MEMBERS = C // G
EPSILON = 1e-06
MESH = pl.DeviceIdType.MESH
F32 = jnp.float32
BF16 = jnp.bfloat16


def plan_of(tm, height, frames, rows, columns):
    s = types.SimpleNamespace()
    s.tm, s.nz = tm, height
    s.nyx = tm // 2
    s.nx = 4 if s.nyx >= 16 else 2
    s.ny = s.nyx // s.nx
    s.frames, s.rows, s.columns = frames, rows, columns
    s.stages = (s.nz, 2 * s.nx, s.ny)
    s.taps = 28
    s.half = s.taps * C // 2
    s.parts = ((("y", "x", 1024), ("x", "y", s.half - 1024)), (("x", "y", s.half),))
    s.size = {"y": s.ny, "x": s.nx}
    s.kept = s.half // s.nyx
    s.z_rows = 16 * -(-s.kept // 16 // s.nz)
    return s


def bundle(sem, ref):
    pltpu.make_async_copy(ref, ref, sem).wait()


def group_total(row):
    lane = lax.broadcasted_iota(jnp.int32, row.shape, 1)
    for step in (1, 2):
        ahead = pltpu.roll(row, C - step, 1)
        behind = pltpu.roll(row, step, 1)
        row = row + jnp.where(lane & step == 0, ahead, behind)
    return row


def wrap(i, n):
    return jnp.where(i >= n, i - n, i)


def sigmoid(u):
    return 1.0 / (1.0 + jnp.exp(-u))


class Place:
    def __init__(self, s):
        self.s = s
        self.tm = tm = lax.axis_index("tm")
        self.z = z = lax.axis_index("height")
        self.core = core = tm % 2
        self.yx = yx = tm // 2
        self.x = yx % s.nx
        self.y = yx // s.nx
        self.mate_tm = mate_tm = tm + 1 - 2 * core
        self.z_ring = z_ring = [z] + [wrap(z + d, s.nz) for d in range(1, s.nz)]
        self.x_ring = [self.x] + [wrap(self.x + d, s.nx) for d in range(1, s.nx)]
        self.y_ring = [self.y] + [wrap(self.y + d, s.ny) for d in range(1, s.ny)]
        self.rings = {"y": self.y_ring, "x": self.x_ring}
        self.row = [self.tm_of(self.y, q, core) for q in self.x_ring]
        self.column = [self.tm_of(q, self.x, core) for q in self.y_ring]
        self.lines = {"y": self.column, "x": self.row}
        self.groups = (
            (z, [(tm, q) for q in z_ring[1:]]),
            (self.x * 2 + core, [(mate_tm, z)] + [(q, z) for q in self.row[1:]]
             + [(q + 1 - 2 * core, z) for q in self.row[1:]]),
            (self.y, [(q, z) for q in self.column[1:]]),
        )
        self.tm_next, self.tm_prev = wrap(tm + 1, s.tm), wrap(tm + s.tm - 1, s.tm)
        self.z_next, self.z_prev = z_ring[1], z_ring[-1]
        self.partners = [peer for _, peers in self.groups for peer in peers]
        self.partners = self.partners + [
            (t, q) for t in (self.tm_next, self.tm_prev) for q in (z, self.z_next, self.z_prev)
        ]

    def tm_of(self, y, x, core):
        return (y * self.s.nx + x) * 2 + core

    def greet(self):
        barrier = pltpu.get_barrier_semaphore()
        for partner in self.partners:
            pl.semaphore_signal(barrier, inc=1, device_id=partner, device_id_type=MESH)

    def meet(self):
        pl.semaphore_wait(pltpu.get_barrier_semaphore(), len(self.partners))

    def own_block(self, ref, lo):
        return ref.at[pl.ds(lo, self.s.frames), pl.ds(1, self.s.rows)]

    def own(self, ref):
        return ref[...].astype(F32).reshape(-1, C)

    def bind(self, ar, ar_send, ar_recv, halo_send, halo_recv):
        self.ar, self.ar_send, self.ar_recv = ar, ar_send, ar_recv
        self.halo_send, self.halo_recv = halo_send, halo_recv

    def ar_start(self, k, stage, payload):
        i = 3 * k + stage
        slot, peers = self.groups[stage]
        self.ar[i, slot, 0:1] = payload[0]
        self.ar[i, slot, 1:2] = payload[1]
        for peer in peers:
            pltpu.make_async_remote_copy(
                src_ref=self.ar.at[i, slot],
                dst_ref=self.ar.at[i, slot],
                send_sem=self.ar_send.at[i],
                recv_sem=self.ar_recv.at[i],
                device_id=peer,
                device_id_type=MESH,
            ).start()

    def ar_wait(self, k, stage):
        i = 3 * k + stage
        n = self.s.stages[stage]
        bundle(self.ar_recv.at[i], self.ar.at[i, pl.ds(0, n - 1)])
        parts = [self.ar[i, j] for j in range(n)]
        return [p[0:1] for p in parts], [p[1:2] for p in parts]

    def ar_sent(self, k):
        for stage, n in enumerate(self.s.stages):
            i = 3 * k + stage
            bundle(self.ar_send.at[i], self.ar.at[i, pl.ds(0, n - 1)])

    def local_count(self):
        return float(self.s.frames * self.s.rows * self.s.columns * MEMBERS)

    def local_stats(self, v):
        centre = group_total(jnp.sum(v, axis=0, keepdims=True)) / self.local_count()
        spread = group_total(jnp.sum((v - centre) ** 2, axis=0, keepdims=True))
        return centre, spread

    def join_stats(self, parts, count):
        means, spreads = parts
        centre = sum(means) / float(len(means))
        spread = sum(spreads) + count * sum((mean - centre) ** 2 for mean in means)
        return centre, spread

    def stats_stage(self, k, stage):
        count = self.local_count()
        for n in self.s.stages[:stage]:
            count = count * n
        joined = self.join_stats(self.ar_wait(k, stage), count)
        if stage < 2:
            return self.ar_start(k, stage + 1, joined)
        centre, spread = joined
        return centre, lax.rsqrt(spread / (count * self.s.stages[stage]) + EPSILON)

    def sums_stage(self, k, stage):
        first, second = self.ar_wait(k, stage)
        totals = sum(first), sum(second)
        return totals if stage == 2 else self.ar_start(k, stage + 1, totals)

    def halo_start(self, q, ref, ahead):
        F, R, z = self.s.frames, self.s.rows, self.z
        target = self.tm_next if ahead else self.tm_prev
        far, near = (0, 2) if ahead else (2, 0)
        frames = pl.ds(near, F)
        everything = ref.at[frames, pl.ds(1, R)]
        top, bottom = ref.at[frames, pl.ds(1, 1)], ref.at[frames, pl.ds(R, 1)]
        copies = [
            (everything, ref.at[pl.ds(far, F), pl.ds(1, R)], (target, z)),
            (top, ref.at[pl.ds(near, F), pl.ds(R + 1, 1)], (self.tm, self.z_prev)),
            (bottom, ref.at[pl.ds(near, F), pl.ds(0, 1)], (self.tm, self.z_next)),
            (top, ref.at[pl.ds(far, F), pl.ds(R + 1, 1)], (target, self.z_prev)),
            (bottom, ref.at[pl.ds(far, F), pl.ds(0, 1)], (target, self.z_next)),
        ]
        for piece, place, device in copies:
            pltpu.make_async_remote_copy(
                src_ref=piece,
                dst_ref=place,
                send_sem=self.halo_send.at[q],
                recv_sem=self.halo_recv.at[q],
                device_id=device,
                device_id_type=MESH,
            ).start()

    def halo_bytes(self, sem, ref):
        F, R = self.s.frames, self.s.rows
        bundle(sem, ref.at[pl.ds(0, F + 2), pl.ds(0, F * (R + 4) // (F + 2))])

    def halo_wait(self, q, ref):
        self.halo_bytes(self.halo_recv.at[q], ref)

    def halo_sent(self, q, ref):
        self.halo_bytes(self.halo_send.at[q], ref)


def blank_next(place, ref):
    F = place.s.frames

    @pl.when(place.tm == place.s.tm - 1)
    def _():
        ref[F : F + 2] = jnp.zeros((2,) + ref.shape[1:], ref.dtype)


def copy_first(place, ref):
    @pl.when(place.tm == 0)
    def _():
        ref[0] = ref[2]
        ref[1] = ref[2]


def kernel(
    s,
    x_hbm,
    u_hbm,
    w1_hbm,
    w2_hbm,
    g1_hbm,
    s1_hbm,
    g2_hbm,
    s2_hbm,
    out_hbm,
    ig_hbm,
    wo1_hbm,
    wo2_hbm,
    gg1_hbm,
    sg1_hbm,
    gg2_hbm,
    sg2_hbm,
    w1_ref,
    w2_ref,
    vectors,
    out_ref,
    ig_ref,
    wo,
    results,
    xe,
    ue,
    he,
    ge,
    a1,
    a2,
    g3,
    dact,
    pre_buf,
    ar,
    wg,
    r1,
    p1,
    p3,
    r4,
    zt,
    arrivals,
    ar_send,
    ar_recv,
    halo_send,
    halo_recv,
    w_send,
    w_recv,
    load_sem,
    store_sem,
):
    F, R, W = s.frames, s.rows, s.columns
    E, RE = F + 2, R + 2
    cells = R * W
    place = Place(s)
    place.bind(ar, ar_send, ar_recv, halo_send, halo_recv)
    tm, z, x, y, core = place.tm, place.z, place.x, place.y, place.core
    mate_tm, z_ring = place.mate_tm, place.z_ring

    x_ref, u_ref = place.own_block(xe, 2), place.own_block(ue, 0)
    loads = [
        (x_hbm, x_ref),
        (u_hbm, u_ref),
        (w1_hbm, w1_ref),
        (w2_hbm, w2_ref),
        (g1_hbm, vectors.at[0]),
        (s1_hbm, vectors.at[1]),
        (g2_hbm, vectors.at[2]),
        (s2_hbm, vectors.at[3]),
    ]
    loads = [pltpu.make_async_copy(a, b, load_sem.at[i]) for i, (a, b) in enumerate(loads)]
    for load in loads:
        load.start()
    place.greet()

    def shifted(v, dst, f):
        column = lax.broadcasted_iota(jnp.int32, v.shape, 0) & (W - 1)
        left = jnp.where(column == 0, 0.0, pltpu.roll(v, 1, 0))
        right = jnp.where(column == W - 1, 0.0, pltpu.roll(v, RE * W - 1, 0))
        for k, piece in enumerate((left, v, right)):
            dst[f, :, :, k * C : (k + 1) * C] = piece.astype(BF16).reshape(RE, W, C)

    def blank_rows(dst):
        blank = jnp.zeros((E, 1) + dst.shape[2:], dst.dtype)

        @pl.when(z == 0)
        def _():
            dst[:, 0:1] = blank

        @pl.when(z == s.nz - 1)
        def _():
            dst[:, R + 1 : R + 2] = blank

    def build_act(src, dst, stats, gain, shift):
        centre, inverse = stats
        scale = inverse * gain

        def frame(f, carry):
            v = src[f].astype(F32).reshape(RE * W, C)
            affine = (v - centre) * scale + shift
            shifted(affine * sigmoid(affine), dst, f)
            return carry

        lax.fori_loop(0, E, frame, 0)
        blank_rows(dst)

    def build_grad(src):
        def frame(f, carry):
            shifted(src[f].astype(F32).reshape(RE * W, C), g3, f)
            return carry

        lax.fori_loop(0, E, frame, 0)
        blank_rows(g3)

    def dot(a, b):
        return jnp.dot(a, b, preferred_element_type=F32)

    def dot_lanes(a, b):
        return lax.dot_general(a, b, (((1,), (1,)), ((), ())), preferred_element_type=F32)

    def patches(src, f):
        return jnp.concatenate([src[f, j : j + R].reshape(cells, 3 * C) for j in range(3)], axis=1)

    def conv(src, weight):
        taps = [weight[9 * i : 9 * i + 9].reshape(9 * C, C) for i in range(3)]
        first = dot(patches(src, 0), taps[0])
        second = None
        for f in (1, 2):
            both = dot(patches(src, f), jnp.concatenate([taps[f], taps[f - 1]], axis=1))
            first = first + both[:, :C]
            second = both[:, C:] if second is None else second + both[:, C:]
        return first, second + dot(patches(src, 3), taps[2])

    def back_conv(src, weight):
        def flipped(i):
            return jnp.concatenate([weight[9 * i + 8 - jk] for jk in range(9)], axis=1)

        def pair(i):
            return jnp.concatenate([flipped(i), flipped(i + 1)], axis=0)

        first = dot_lanes(patches(src, 0), flipped(2))
        second = None
        for f in (1, 2):
            both = dot_lanes(patches(src, f), pair(2 - f))
            first = first + both[:, :C]
            second = both[:, C:] if second is None else second + both[:, C:]
        dact[0] = first
        dact[1] = second + dot_lanes(patches(src, 3), flipped(0))

        @pl.when(tm == 0)
        def _():
            both = dot_lanes(patches(src, 0), pair(0))
            dact[0] += both[:, :C] + both[:, C:] + dot_lanes(patches(src, 1), flipped(0))

    def weight_grad(act, grad, q):
        turned = [grad[f].reshape(cells, C).T for f in range(F)]
        both = jnp.concatenate(turned, axis=0)
        wg[q, 14 * C : 15 * C, :] = jnp.zeros((C, C), BF16)
        mate = (mate_tm, z)

        def row_tap(j, base):
            window = [act[f, pl.ds(j, R)].reshape(cells, 3 * C) for f in range(E)]
            one, two = dot(both, window[1]), dot(both, window[2])
            sums = (
                dot(turned[0], window[0]) + one[C:],
                one[:C] + two[C:],
                two[:C] + dot(turned[1], window[3]),
            )
            for i, total in enumerate(sums):
                total = total.astype(BF16)
                for k in range(3):
                    at = 3 * i + k
                    lo = base(at) * C
                    wg[q, pl.ds(pl.multiple_of(lo, C), C), :] = total[:, k * C : (k + 1) * C].T

        def send(i, src, dst, taps):
            pltpu.make_async_remote_copy(
                src_ref=wg.at[q, pl.ds(pl.multiple_of(src * C, C), taps * C)],
                dst_ref=r1.at[q, pl.ds(pl.multiple_of(dst * C, C), taps * C)],
                send_sem=w_send.at[q, i],
                recv_sem=w_recv.at[q, i],
                device_id=mate,
                device_id_type=MESH,
            ).start()

        row_tap(2 - 2 * core, lambda at: (1 - core) * 19 + at)
        send(0, (1 - core) * 19, (1 - core) * 5, 9)
        row_tap(1, lambda at: 9 + at if at < 5 else 10 + at)
        send(1, 14 - core * 5, core * 9, 5)
        row_tap(2 * core, lambda at: core * 19 + at)

    def norm_back_sums(values, stats, gain, shift):
        centre, inverse = stats
        total_cross = jnp.zeros((1, C), F32)
        total = jnp.zeros((1, C), F32)
        for f in range(F):
            normed = (values[f].astype(F32).reshape(cells, C) - centre) * inverse
            affine = normed * gain + shift
            sig = sigmoid(affine)
            pre = dact[f] * sig * (1.0 + affine * (1.0 - sig))
            pre_buf[f] = pre
            total_cross += jnp.sum(pre * normed, axis=0, keepdims=True)
            total += jnp.sum(pre, axis=0, keepdims=True)
        return total_cross, total

    def norm_back_value(values, stats, gain, sums, f):
        centre, inverse = stats
        gain_grad, shift_grad = sums
        members = float(F * cells * MEMBERS * s.tm * s.nz)
        mean_grad = group_total(gain * shift_grad) / members
        mean_cross = group_total(gain * gain_grad) / members
        normed = (values[f].astype(F32).reshape(cells, C) - centre) * inverse
        return inverse * (pre_buf[f] * gain - mean_grad - normed * mean_cross)

    def weight_reduce(q, home, arrivals):
        out = wo.at[q]
        mate = (mate_tm, z)
        mine = core * s.half
        spot = {"y": y, "x": x}
        parts = []
        lo = at = kept = 0
        for p, (first, second, rows) in enumerate(s.parts[q]):
            part = types.SimpleNamespace(p=p, first=first, second=second, lo=lo, at=at, kept=kept)
            part.one = rows // s.size[first]
            part.two = part.one // s.size[second]
            part.r2, part.r3 = arrivals[2 * p], arrivals[2 * p + 1]
            lo, at, kept = lo + rows, at + part.one, kept + part.two
            parts.append(part)

        def span(lo, rows):
            return pl.ds(pl.multiple_of(lo, 16), rows)

        def send(i, src, dst, device):
            pltpu.make_async_remote_copy(
                src_ref=src,
                dst_ref=dst,
                send_sem=w_send.at[q, i],
                recv_sem=w_recv.at[q, i],
                device_id=device,
                device_id_type=MESH,
            ).start()

        def arrived(i, rows):
            bundle(w_recv.at[q, i], wg.at[q, pl.ds(0, rows)])

        def sent(i, rows):
            bundle(w_send.at[q, i], wg.at[q, pl.ds(0, rows)])

        def scatter(i, src, lo, rows, dst, axis):
            for d in range(1, s.size[axis]):
                to = place.rings[axis][d]
                device = (place.lines[axis][d], z)
                send(i, src.at[q, span(lo + to * rows, rows)], dst.at[spot[axis]], device)

        def gather_sum(src, lo, rows, dst, axis):
            total = src[q, span(lo + spot[axis] * rows, rows)].astype(F32)
            for d in range(1, s.size[axis]):
                total += dst[place.rings[axis][d]].astype(F32)
            return total.astype(BF16)

        def step_one():
            arrived(0, 9 * C)
            arrived(1, 5 * C)

            def piece(t, carry):
                rows = span(t * C, C)
                kept = wg[q, span(mine + t * C, C)].astype(F32)
                p1[q, rows] = (kept + r1[q, rows].astype(F32)).astype(BF16)
                return carry

            for part in parts:
                rows = part.one * s.size[part.first]
                lax.fori_loop(part.lo // C, (part.lo + rows) // C, piece, 0)
                scatter(2 + part.p, p1, part.lo, part.one, part.r2, part.first)

        def step_two():
            for part in parts:
                arrived(2 + part.p, (s.size[part.first] - 1) * part.one)
                r1[q, part.at : part.at + part.one] = gather_sum(
                    p1, part.lo, part.one, part.r2, part.first
                )
                scatter(4 + part.p, r1, part.at, part.two, part.r3, part.second)

        def step_three():
            for part in parts:
                arrived(4 + part.p, (s.size[part.second] - 1) * part.two)
                p3[q, part.kept : part.kept + part.two] = gather_sum(
                    r1, part.at, part.two, part.r3, part.second
                )
            spare = s.nz * s.z_rows - s.kept
            if spare:
                p3[q, s.kept :] = jnp.zeros((spare, C), BF16)
            for to in z_ring[1:]:
                send(6, p3.at[q, span(to * s.z_rows, s.z_rows)], r4.at[q, z], (tm, to))

        def step_four():
            arrived(6, (s.nz - 1) * s.z_rows)
            lo = span(z * s.z_rows, s.z_rows)
            total = p3[q, lo].astype(F32)
            for other in z_ring[1:]:
                total += r4[q, other].astype(F32)
            zt[q, lo] = total.astype(BF16)
            for to in z_ring[1:]:
                send(7, zt.at[q, lo], zt.at[q, lo], (tm, to))

        def chunk(part, first, second=None):
            lo = mine + part.lo + first * part.one
            return span(lo, part.one) if second is None else span(lo + second * part.two, part.two)

        def spread(i, rows, axis, each):
            for d in range(1, s.size[axis]):
                device = (place.lines[axis][d], z)
                send(i + (d - 1 if each else 0), out.at[rows], out.at[rows], device)

        def step_five():
            arrived(7, (s.nz - 1) * s.z_rows)
            for part in parts:
                rows = chunk(part, spot[part.first], spot[part.second])
                out[rows] = zt[q, part.kept : part.kept + part.two]
                spread(8 + part.p, rows, part.second, False)

        def deliver(rows):
            send(10, out.at[rows], home.at[rows], mate)

        def step_six():
            for part in parts:
                arrived(8 + part.p, (s.size[part.second] - 1) * part.two)
                rows = chunk(part, spot[part.first])
                spread(11 + 3 * part.p, rows, part.first, True)
            if len(parts) > 1:
                for part in parts:
                    deliver(chunk(part, spot[part.first]))

        def keep():
            return pltpu.make_async_copy(
                out.at[span(mine, s.half)], home.at[span(mine, s.half)], store_sem.at[6 + q]
            )

        def step_seven():
            for d in (1, 3, 2):
                for part in parts:
                    n = s.size[part.first]
                    if d < n:
                        arrived(11 + 3 * part.p + d - 1, part.one)
                        if len(parts) > 1:
                            deliver(chunk(part, place.rings[part.first][n - d]))
            if len(parts) == 1:
                deliver(span(mine, s.half))
            keep().start()

        def step_eight():
            arrived(10, s.half)
            keep().wait()

        def finish():
            sent(0, 9 * C)
            sent(1, 5 * C)
            for part in parts:
                first, second = s.size[part.first], s.size[part.second]
                sent(2 + part.p, (first - 1) * part.one)
                sent(4 + part.p, (second - 1) * part.two)
                sent(8 + part.p, (second - 1) * part.two)
                for d in range(1, first):
                    sent(11 + 3 * part.p + d - 1, part.one)
            sent(6, (s.nz - 1) * s.z_rows)
            sent(7, (s.nz - 1) * s.z_rows)
            sent(10, s.half)

        return [
            None,
            step_one,
            step_two,
            step_three,
            step_four,
            step_five,
            step_six,
            step_seven,
            step_eight,
            finish,
        ]

    def store(i, src, dst):
        copy = pltpu.make_async_copy(src, dst, store_sem.at[i])
        copy.start()
        return copy

    loads[0].wait()
    payload = place.local_stats(place.own(x_ref))
    place.meet()
    place.ar_start(0, 0, payload)
    place.halo_start(0, xe, True)
    loads[1].wait()
    place.halo_start(1, ue, False)
    place.stats_stage(0, 0)
    for load in loads[2:]:
        load.wait()
    gain1, shift1, gain2, shift2 = (vectors[i] for i in range(4))
    place.stats_stage(0, 1)
    place.halo_wait(0, xe)
    copy_first(place, xe)
    place.halo_wait(1, ue)
    blank_next(place, ue)
    stats1 = place.stats_stage(0, 2)

    build_act(xe, a1, stats1, gain1, shift1)
    for f, value in enumerate(conv(a1, w1_ref)):
        he[2 + f, 1 : R + 1] = value.astype(BF16).reshape(R, W, C)
    hidden = place.own_block(he, 2)
    place.ar_start(1, 0, place.local_stats(place.own(hidden)))
    build_grad(ue)
    place.stats_stage(1, 0)
    place.halo_start(2, he, True)
    back_conv(g3, w2_ref)
    place.stats_stage(1, 1)
    place.halo_wait(2, he)
    copy_first(place, he)
    stats2 = place.stats_stage(1, 2)

    second = weight_reduce(1, wo2_hbm, arrivals[4:])
    first = weight_reduce(0, wo1_hbm, arrivals[:4])
    place.ar_start(2, 0, norm_back_sums(hidden, stats2, gain2, shift2))
    build_act(he, a2, stats2, gain2, shift2)
    place.sums_stage(2, 0)
    weight_grad(a2, u_ref, 1)
    place.sums_stage(2, 1)
    second[1]()
    sums2 = place.sums_stage(2, 2)
    for f in range(F):
        value = norm_back_value(hidden, stats2, gain2, sums2, f)
        ge[f, 1 : R + 1] = value.astype(BF16).reshape(R, W, C)
    place.halo_start(3, ge, False)
    weight_grad(a1, place.own_block(ge, 0), 0)
    first[1]()
    second[2]()
    place.halo_wait(3, ge)
    blank_next(place, ge)
    build_grad(ge)
    back_conv(g3, w1_ref)
    place.ar_start(3, 0, norm_back_sums(x_ref, stats1, gain1, shift1))
    first[2]()
    second[3]()
    place.sums_stage(3, 0)
    branch = conv(a2, w2_ref)
    first[3]()
    place.sums_stage(3, 1)
    for f in range(F):
        total = x_ref[f].astype(F32).reshape(cells, C) + branch[f]
        out_ref[f] = total.astype(BF16).reshape(R, W, C)
    stores = [store(0, out_ref, out_hbm)]
    second[4]()
    first[4]()
    sums1 = place.sums_stage(3, 2)
    second[5]()
    first[5]()
    for f in range(F):
        value = norm_back_value(x_ref, stats1, gain1, sums1, f)
        total = u_ref[f].astype(F32).reshape(cells, C) + value
        ig_ref[f] = total.astype(BF16).reshape(R, W, C)
    stores.append(store(1, ig_ref, ig_hbm))
    second[6]()
    first[6]()
    for i, (row, result) in enumerate(zip(sums1 + sums2, (gg1_hbm, sg1_hbm, gg2_hbm, sg2_hbm))):
        results[i] = row
        stores.append(store(2 + i, results.at[i], result))
    second[7]()
    first[7]()
    second[8]()
    first[8]()

    for copy in stores:
        copy.wait()
    second[9]()
    first[9]()
    for k in range(4):
        place.ar_sent(k)
    for q, ref in enumerate((xe, ue, he, ge)):
        place.halo_sent(q, ref)


def finish_kernel(*refs):
    sources, places, (fields, vectors, narrow, wide, load_sem, sem) = refs[:8], refs[8:16], refs[16:]
    copies = []

    def load(i, src, dst):
        copy = pltpu.make_async_copy(src, dst, load_sem.at[i])
        copy.start()
        return copy

    def write(src, dst):
        copy = pltpu.make_async_copy(src, dst, sem.at[len(copies)])
        copy.start()
        copies.append(copy)

    spans = ((0, 9), (9, 10), (19, 9))
    weights = []
    for j, (lo, count) in enumerate(spans):
        for q in range(2):
            rows = pl.ds(lo * C, count * C)
            weights.append(load(2 * j + q, sources[2 + q].at[rows], narrow.at[q, rows]))
    bounce = [(i, fields.at[i]) for i in range(2)] + [(4 + i, vectors.at[i]) for i in range(4)]
    others = [load(6 + n, sources[i], ref) for n, (i, ref) in enumerate(bounce)]
    for j, (lo, count) in enumerate(spans):
        for q in range(2):
            weights[2 * j + q].wait()
            for i in range(3):
                to = (9 * i + 3 * j) * C
                for k in range(3):
                    at = 3 * i + k
                    tap = lo + at + (1 if count == 10 and at >= 5 else 0)
                    block = narrow[q, tap * C : (tap + 1) * C]
                    wide[q, to + k * C : to + (k + 1) * C] = block.astype(F32)
                rows = pl.ds(to, 3 * C)
                write(wide.at[q, rows], places[2 + q].at[rows])
        if j == 0:
            for copy, (i, ref) in zip(others, bounce):
                copy.wait()
                write(ref, places[i])
    for copy in copies:
        copy.wait()


def body(inputs, gain1, shift1, weight1, gain2, shift2, weight2, upstream):
    F, R, W, _ = inputs.shape
    s = plan_of(lax.axis_size("tm"), lax.axis_size("height"), F, R, W)
    E, RE = F + 2, R + 2
    cells = R * W
    hbm = pl.BlockSpec(memory_space=pltpu.HBM)
    field = jax.ShapeDtypeStruct(inputs.shape, BF16)
    weights = jax.ShapeDtypeStruct((s.taps * C, C), BF16)
    vector = jax.ShapeDtypeStruct((1, C), F32)
    wide = pltpu.VMEM((E, RE, W, C), BF16)
    wider = pltpu.VMEM((E, RE, W, 3 * C), BF16)
    arrivals = []
    for parts in s.parts:
        for first, second, rows in parts:
            one = rows // s.size[first]
            arrivals.append(pltpu.VMEM((s.size[first], one, C), BF16))
            arrivals.append(pltpu.VMEM((s.size[second], one // s.size[second], C), BF16))
    room = 60 * 1024 * 1024
    results = pl.pallas_call(
        functools.partial(kernel, s),
        out_shape=[field, field, weights, weights, vector, vector, vector, vector],
        in_specs=[hbm] * 8,
        out_specs=[hbm] * 8,
        scratch_shapes=[
            pltpu.VMEM((27, C, C), BF16),
            pltpu.VMEM((27, C, C), BF16),
            pltpu.VMEM((4, 1, C), F32),
            pltpu.VMEM((F, R, W, C), BF16),
            pltpu.VMEM((F, R, W, C), BF16),
            pltpu.VMEM((2, s.taps * C, C), BF16),
            pltpu.VMEM((4, 1, C), F32),
            wide,
            wide,
            wide,
            wide,
            wider,
            wider,
            wider,
            pltpu.VMEM((F, cells, C), F32),
            pltpu.VMEM((F, cells, C), F32),
            pltpu.VMEM((12, max(s.stages), 2, C), F32),
            pltpu.VMEM((2, s.taps * C, C), BF16),
            pltpu.VMEM((2, s.half, C), BF16),
            pltpu.VMEM((2, s.half, C), BF16),
            pltpu.VMEM((2, s.nz * s.z_rows, C), BF16),
            pltpu.VMEM((2, s.nz, s.z_rows, C), BF16),
            pltpu.VMEM((2, s.nz * s.z_rows, C), BF16),
            arrivals,
            pltpu.SemaphoreType.DMA((12,)),
            pltpu.SemaphoreType.DMA((12,)),
            pltpu.SemaphoreType.DMA((4,)),
            pltpu.SemaphoreType.DMA((4,)),
            pltpu.SemaphoreType.DMA((2, 17)),
            pltpu.SemaphoreType.DMA((2, 17)),
            pltpu.SemaphoreType.DMA((8,)),
            pltpu.SemaphoreType.DMA((8,)),
        ],
        compiler_params=pltpu.CompilerParams(
            collective_id=0, has_side_effects=True, vmem_limit_bytes=room
        ),
        cost_estimate=pl.CostEstimate(
            flops=6 * 2 * F * cells * 27 * C * C, bytes_accessed=8_000_000, transcendentals=1_000_000
        ),
    )(
        inputs,
        upstream,
        weight1.reshape(27, C, C),
        weight2.reshape(27, C, C),
        gain1.reshape(1, C),
        shift1.reshape(1, C),
        gain2.reshape(1, C),
        shift2.reshape(1, C),
    )
    total = jax.ShapeDtypeStruct((27 * C, C), F32)
    output, input_grad, first, second, gg1, sg1, gg2, sg2 = pl.pallas_call(
        finish_kernel,
        out_shape=[field, field, total, total, vector, vector, vector, vector],
        in_specs=[hbm] * 8,
        out_specs=[hbm] * 8,
        scratch_shapes=[
            pltpu.VMEM((2, F, R, W, C), BF16),
            pltpu.VMEM((4, 1, C), F32),
            pltpu.VMEM((2, s.taps * C, C), BF16),
            pltpu.VMEM((2, 27 * C, C), F32),
            pltpu.SemaphoreType.DMA((12,)),
            pltpu.SemaphoreType.DMA((24,)),
        ],
        compiler_params=pltpu.CompilerParams(vmem_limit_bytes=room),
        cost_estimate=pl.CostEstimate(flops=0, bytes_accessed=6_000_000, transcendentals=0),
    )(*results)
    return (
        output,
        input_grad,
        first.reshape(3, 3, 3, C, C),
        second.reshape(3, 3, 3, C, C),
        gg1.reshape(C),
        sg1.reshape(C),
        gg2.reshape(C),
        sg2.reshape(C),
    )


def solution(mesh):
    fields = P("tm", "height", None, None)
    return jax.shard_map(
        body,
        mesh=mesh,
        in_specs=(fields, P(), P(), P(), P(), P(), P(), fields),
        out_specs=(fields, fields, P(), P(), P(), P(), P(), P()),
        check_vma=False,
    )
```

```python
import functools
import types

import jax
import jax.numpy as jnp
from jax import lax
from jax.experimental import pallas as pl
from jax.experimental.pallas import tpu as pltpu
from jax.sharding import PartitionSpec as P

C = 128
G = 32
MEMBERS = C // G
EPSILON = 1e-06
MESH = pl.DeviceIdType.MESH
F32 = jnp.float32
BF16 = jnp.bfloat16


def plan_of(tm, height, frames, rows, columns):
    s = types.SimpleNamespace()
    s.tm, s.nz = tm, height
    s.nyx = tm // 2
    s.nx = 4 if s.nyx >= 16 else 2
    s.ny = s.nyx // s.nx
    s.frames, s.rows, s.columns = frames, rows, columns
    s.stages = (2 * s.nz, s.nyx)
    s.taps = 28
    s.half = s.taps * C // 2
    s.parts = ((("x", "y", 1024), ("y", "x", s.half - 1024)), (("y", "x", s.half),))
    s.size = {"y": s.ny, "x": s.nx}
    s.kept = s.half // s.nyx
    s.z_rows = 16 * -(-s.kept // 16 // s.nz)
    return s


def bundle(sem, ref):
    pltpu.make_async_copy(ref, ref, sem).wait()


def group_total(row):
    lane = lax.broadcasted_iota(jnp.int32, row.shape, 1)
    for step in (1, 2):
        ahead = pltpu.roll(row, C - step, 1)
        behind = pltpu.roll(row, step, 1)
        row = row + jnp.where(lane & step == 0, ahead, behind)
    return row


def wrap(i, n):
    return jnp.where(i >= n, i - n, i)


def sigmoid(u):
    return 1.0 / (1.0 + jnp.exp(-u))


class Place:
    def __init__(self, s):
        self.s = s
        self.tm = tm = lax.axis_index("tm")
        self.z = z = lax.axis_index("height")
        self.core = core = tm % 2
        self.yx = yx = tm // 2
        self.x = yx % s.nx
        self.y = yx // s.nx
        self.mate_tm = mate_tm = tm + 1 - 2 * core
        self.z_ring = z_ring = [z] + [wrap(z + d, s.nz) for d in range(1, s.nz)]
        self.x_ring = [self.x] + [wrap(self.x + d, s.nx) for d in range(1, s.nx)]
        self.y_ring = [self.y] + [wrap(self.y + d, s.ny) for d in range(1, s.ny)]
        self.rings = {"y": self.y_ring, "x": self.x_ring}
        self.row = [self.tm_of(self.y, q, core) for q in self.x_ring]
        self.column = [self.tm_of(q, self.x, core) for q in self.y_ring]
        self.lines = {"y": self.column, "x": self.row}
        self.groups = (
            (core * s.nz + z, [(tm, q) for q in z_ring[1:]] + [(mate_tm, q) for q in z_ring]),
            (yx, [(wrap(yx + d, s.nyx) * 2 + core, z) for d in range(1, s.nyx)]),
        )
        self.tm_next, self.tm_prev = wrap(tm + 1, s.tm), wrap(tm + s.tm - 1, s.tm)
        self.z_next, self.z_prev = z_ring[1], z_ring[-1]
        self.partners = [peer for _, peers in self.groups for peer in peers]
        self.partners = self.partners + [
            (t, q) for t in (self.tm_next, self.tm_prev) for q in (z, self.z_next, self.z_prev)
        ]

    def tm_of(self, y, x, core):
        return (y * self.s.nx + x) * 2 + core

    def greet(self):
        barrier = pltpu.get_barrier_semaphore()
        for partner in self.partners:
            pl.semaphore_signal(barrier, inc=1, device_id=partner, device_id_type=MESH)

    def meet(self):
        pl.semaphore_wait(pltpu.get_barrier_semaphore(), len(self.partners))

    def own_block(self, ref, lo):
        return ref.at[pl.ds(lo, self.s.frames), pl.ds(1, self.s.rows)]

    def own(self, ref):
        return ref[...].astype(F32).reshape(-1, C)

    def bind(self, ar, ar_send, ar_recv, halo_send, halo_recv):
        self.ar, self.ar_send, self.ar_recv = ar, ar_send, ar_recv
        self.halo_send, self.halo_recv = halo_send, halo_recv

    def ar_start(self, k, stage, payload):
        i = 2 * k + stage
        slot, peers = self.groups[stage]
        self.ar[i, slot, 0:1] = payload[0]
        self.ar[i, slot, 1:2] = payload[1]
        for peer in peers:
            pltpu.make_async_remote_copy(
                src_ref=self.ar.at[i, slot],
                dst_ref=self.ar.at[i, slot],
                send_sem=self.ar_send.at[i],
                recv_sem=self.ar_recv.at[i],
                device_id=peer,
                device_id_type=MESH,
            ).start()

    def ar_wait(self, k, stage):
        i = 2 * k + stage
        n = self.s.stages[stage]
        bundle(self.ar_recv.at[i], self.ar.at[i, pl.ds(0, n - 1)])
        parts = [self.ar[i, j] for j in range(n)]
        return [p[0:1] for p in parts], [p[1:2] for p in parts]

    def ar_sent(self, k):
        for stage, n in enumerate(self.s.stages):
            i = 2 * k + stage
            bundle(self.ar_send.at[i], self.ar.at[i, pl.ds(0, n - 1)])

    def local_count(self):
        return float(self.s.frames * self.s.rows * self.s.columns * MEMBERS)

    def local_stats(self, v):
        centre = group_total(jnp.sum(v, axis=0, keepdims=True)) / self.local_count()
        spread = group_total(jnp.sum((v - centre) ** 2, axis=0, keepdims=True))
        return centre, spread

    def join_stats(self, parts, count):
        means, spreads = parts
        centre = sum(means) / float(len(means))
        spread = sum(spreads) + count * sum((mean - centre) ** 2 for mean in means)
        return centre, spread

    def stats_stage(self, k, stage):
        count = self.local_count()
        for n in self.s.stages[:stage]:
            count = count * n
        joined = self.join_stats(self.ar_wait(k, stage), count)
        if stage < 1:
            return self.ar_start(k, stage + 1, joined)
        centre, spread = joined
        return centre, lax.rsqrt(spread / (count * self.s.stages[stage]) + EPSILON)

    def sums_stage(self, k, stage):
        first, second = self.ar_wait(k, stage)
        totals = sum(first), sum(second)
        return totals if stage == 1 else self.ar_start(k, stage + 1, totals)

    def halo_start(self, q, ref, ahead):
        F, R, z = self.s.frames, self.s.rows, self.z
        target = self.tm_next if ahead else self.tm_prev
        far, near = (0, 2) if ahead else (2, 0)
        frames = pl.ds(near, F)
        everything = ref.at[frames, pl.ds(1, R)]
        top, bottom = ref.at[frames, pl.ds(1, 1)], ref.at[frames, pl.ds(R, 1)]
        copies = [
            (everything, ref.at[pl.ds(far, F), pl.ds(1, R)], (target, z)),
            (top, ref.at[pl.ds(near, F), pl.ds(R + 1, 1)], (self.tm, self.z_prev)),
            (bottom, ref.at[pl.ds(near, F), pl.ds(0, 1)], (self.tm, self.z_next)),
            (top, ref.at[pl.ds(far, F), pl.ds(R + 1, 1)], (target, self.z_prev)),
            (bottom, ref.at[pl.ds(far, F), pl.ds(0, 1)], (target, self.z_next)),
        ]
        for piece, place, device in copies:
            pltpu.make_async_remote_copy(
                src_ref=piece,
                dst_ref=place,
                send_sem=self.halo_send.at[q],
                recv_sem=self.halo_recv.at[q],
                device_id=device,
                device_id_type=MESH,
            ).start()

    def halo_bytes(self, sem, ref):
        F, R = self.s.frames, self.s.rows
        bundle(sem, ref.at[pl.ds(0, F + 2), pl.ds(0, F * (R + 4) // (F + 2))])

    def halo_wait(self, q, ref):
        self.halo_bytes(self.halo_recv.at[q], ref)

    def halo_sent(self, q, ref):
        self.halo_bytes(self.halo_send.at[q], ref)


def blank_next(place, ref):
    F = place.s.frames

    @pl.when(place.tm == place.s.tm - 1)
    def _():
        ref[F : F + 2] = jnp.zeros((2,) + ref.shape[1:], ref.dtype)


def copy_first(place, ref):
    @pl.when(place.tm == 0)
    def _():
        ref[0] = ref[2]
        ref[1] = ref[2]


def kernel(
    s,
    x_hbm,
    u_hbm,
    w1_hbm,
    w2_hbm,
    g1_hbm,
    s1_hbm,
    g2_hbm,
    s2_hbm,
    out_hbm,
    ig_hbm,
    wo1_hbm,
    wo2_hbm,
    gg1_hbm,
    sg1_hbm,
    gg2_hbm,
    sg2_hbm,
    w1_ref,
    w2_ref,
    wf1,
    wf2,
    vectors,
    out_ref,
    ig_ref,
    wo,
    results,
    xe,
    ue,
    he,
    ge,
    a1,
    a2,
    g3,
    dact,
    pre_buf,
    ar,
    wg,
    r1,
    p1,
    p3,
    r4,
    zt,
    arrivals,
    ar_send,
    ar_recv,
    halo_send,
    halo_recv,
    w_send,
    w_recv,
    load_sem,
    store_sem,
):
    F, R, W = s.frames, s.rows, s.columns
    E, RE = F + 2, R + 2
    cells = R * W
    place = Place(s)
    place.bind(ar, ar_send, ar_recv, halo_send, halo_recv)
    tm, z, x, y, core = place.tm, place.z, place.x, place.y, place.core
    mate_tm, z_ring = place.mate_tm, place.z_ring

    x_ref, u_ref = place.own_block(xe, 2), place.own_block(ue, 0)
    loads = [
        (x_hbm, x_ref),
        (u_hbm, u_ref),
        (w1_hbm, w1_ref),
        (w2_hbm, w2_ref),
        (g1_hbm, vectors.at[0]),
        (s1_hbm, vectors.at[1]),
        (g2_hbm, vectors.at[2]),
        (s2_hbm, vectors.at[3]),
    ]
    loads = [pltpu.make_async_copy(a, b, load_sem.at[i]) for i, (a, b) in enumerate(loads)]
    for load in loads:
        load.start()
    place.greet()

    def shifted(v, dst, f):
        column = lax.broadcasted_iota(jnp.int32, v.shape, 0) & (W - 1)
        left = jnp.where(column == 0, 0.0, pltpu.roll(v, 1, 0))
        right = jnp.where(column == W - 1, 0.0, pltpu.roll(v, RE * W - 1, 0))
        for k, piece in enumerate((left, v, right)):
            dst[f, :, :, k * C : (k + 1) * C] = piece.astype(BF16).reshape(RE, W, C)

    def blank_rows(dst):
        blank = jnp.zeros((E, 1) + dst.shape[2:], dst.dtype)

        @pl.when(z == 0)
        def _():
            dst[:, 0:1] = blank

        @pl.when(z == s.nz - 1)
        def _():
            dst[:, R + 1 : R + 2] = blank

    def build_act(src, dst, stats, gain, shift):
        centre, inverse = stats
        scale = inverse * gain

        def frame(f, carry):
            v = src[f].astype(F32).reshape(RE * W, C)
            affine = (v - centre) * scale + shift
            shifted(affine * sigmoid(affine), dst, f)
            return carry

        lax.fori_loop(0, E, frame, 0)
        blank_rows(dst)

    def build_grad(src):
        def frame(f, carry):
            shifted(src[f].astype(F32).reshape(RE * W, C), g3, f)
            return carry

        lax.fori_loop(0, E, frame, 0)
        blank_rows(g3)

    def dot(a, b):
        return jnp.dot(a, b, preferred_element_type=F32)

    def turn(src, dst):
        for at in range(27):
            dst[at // 9, (at % 9) * C : (at % 9 + 1) * C, :] = src[26 - at].T

    def patches(src, f):
        return jnp.concatenate([src[f, j : j + R].reshape(cells, 3 * C) for j in range(3)], axis=1)

    def conv(src, taps):
        first = dot(patches(src, 0), taps[0])
        second = None
        for f in (1, 2):
            both = dot(patches(src, f), jnp.concatenate([taps[f], taps[f - 1]], axis=1))
            first = first + both[:, :C]
            second = both[:, C:] if second is None else second + both[:, C:]
        return first, second + dot(patches(src, 3), taps[2])

    def taps_of(weight):
        return [weight[9 * i : 9 * i + 9].reshape(9 * C, C) for i in range(3)]

    def back_conv(src, weight):
        dact[0], dact[1] = conv(src, [weight[i] for i in range(3)])

    def back_first(src, weight):
        @pl.when(tm == 0)
        def _():
            both = dot(patches(src, 0), jnp.concatenate([weight[1], weight[2]], axis=1))
            dact[0] += both[:, :C] + both[:, C:] + dot(patches(src, 1), weight[2])

    def weight_grad(act, grad, q):
        turned = [grad[f].reshape(cells, C).T for f in range(F)]
        both = jnp.concatenate(turned, axis=0)
        wg[q, 14 * C : 15 * C, :] = jnp.zeros((C, C), BF16)
        mate = (mate_tm, z)

        def row_tap(j, base):
            window = [act[f, pl.ds(j, R)].reshape(cells, 3 * C) for f in range(E)]
            one, two = dot(both, window[1]), dot(both, window[2])
            sums = (
                dot(turned[0], window[0]) + one[C:],
                one[:C] + two[C:],
                two[:C] + dot(turned[1], window[3]),
            )
            for i, total in enumerate(sums):
                total = total.astype(BF16)
                for k in range(3):
                    at = 3 * i + k
                    lo = base(at) * C
                    wg[q, pl.ds(pl.multiple_of(lo, C), C), :] = total[:, k * C : (k + 1) * C].T

        def send(i, src, dst, taps):
            pltpu.make_async_remote_copy(
                src_ref=wg.at[q, pl.ds(pl.multiple_of(src * C, C), taps * C)],
                dst_ref=r1.at[q, pl.ds(pl.multiple_of(dst * C, C), taps * C)],
                send_sem=w_send.at[q, i],
                recv_sem=w_recv.at[q, i],
                device_id=mate,
                device_id_type=MESH,
            ).start()

        row_tap(2 - 2 * core, lambda at: (1 - core) * 19 + at)
        send(0, (1 - core) * 19, (1 - core) * 5, 9)
        row_tap(1, lambda at: 9 + at if at < 5 else 10 + at)
        send(1, 14 - core * 5, core * 9, 5)
        row_tap(2 * core, lambda at: core * 19 + at)

    def norm_back_sums(values, stats, gain, shift):
        centre, inverse = stats
        total_cross = jnp.zeros((1, C), F32)
        total = jnp.zeros((1, C), F32)
        for f in range(F):
            normed = (values[f].astype(F32).reshape(cells, C) - centre) * inverse
            affine = normed * gain + shift
            sig = sigmoid(affine)
            pre = dact[f] * sig * (1.0 + affine * (1.0 - sig))
            pre_buf[f] = pre
            total_cross += jnp.sum(pre * normed, axis=0, keepdims=True)
            total += jnp.sum(pre, axis=0, keepdims=True)
        return total_cross, total

    def norm_back_value(values, stats, gain, sums, f):
        centre, inverse = stats
        gain_grad, shift_grad = sums
        members = float(F * cells * MEMBERS * s.tm * s.nz)
        mean_grad = group_total(gain * shift_grad) / members
        mean_cross = group_total(gain * gain_grad) / members
        normed = (values[f].astype(F32).reshape(cells, C) - centre) * inverse
        return inverse * (pre_buf[f] * gain - mean_grad - normed * mean_cross)

    def weight_reduce(q, home, arrivals):
        out = wo.at[q]
        mate = (mate_tm, z)
        mine = core * s.half
        spot = {"y": y, "x": x}
        parts = []
        lo = at = kept = 0
        for p, (first, second, rows) in enumerate(s.parts[q]):
            part = types.SimpleNamespace(p=p, first=first, second=second, lo=lo, at=at, kept=kept)
            part.one = rows // s.size[first]
            part.two = part.one // s.size[second]
            part.r2, part.r3 = arrivals[2 * p], arrivals[2 * p + 1]
            lo, at, kept = lo + rows, at + part.one, kept + part.two
            parts.append(part)

        def span(lo, rows):
            return pl.ds(pl.multiple_of(lo, 16), rows)

        def send(i, src, dst, device):
            pltpu.make_async_remote_copy(
                src_ref=src,
                dst_ref=dst,
                send_sem=w_send.at[q, i],
                recv_sem=w_recv.at[q, i],
                device_id=device,
                device_id_type=MESH,
            ).start()

        def arrived(i, rows):
            bundle(w_recv.at[q, i], wg.at[q, pl.ds(0, rows)])

        def sent(i, rows):
            bundle(w_send.at[q, i], wg.at[q, pl.ds(0, rows)])

        def scatter(i, src, lo, rows, dst, axis):
            for d in range(1, s.size[axis]):
                to = place.rings[axis][d]
                device = (place.lines[axis][d], z)
                send(i, src.at[q, span(lo + to * rows, rows)], dst.at[spot[axis]], device)

        def gather_sum(src, lo, rows, dst, axis):
            total = src[q, span(lo + spot[axis] * rows, rows)].astype(F32)
            for d in range(1, s.size[axis]):
                total += dst[place.rings[axis][d]].astype(F32)
            return total.astype(BF16)

        def step_one():
            arrived(0, 9 * C)
            arrived(1, 5 * C)

            def piece(t, carry):
                rows = span(t * C, C)
                kept = wg[q, span(mine + t * C, C)].astype(F32)
                p1[q, rows] = (kept + r1[q, rows].astype(F32)).astype(BF16)
                return carry

            for part in parts:
                rows = part.one * s.size[part.first]
                lax.fori_loop(part.lo // C, (part.lo + rows) // C, piece, 0)
                scatter(2 + part.p, p1, part.lo, part.one, part.r2, part.first)

        def step_two():
            for part in parts:
                arrived(2 + part.p, (s.size[part.first] - 1) * part.one)
                r1[q, part.at : part.at + part.one] = gather_sum(
                    p1, part.lo, part.one, part.r2, part.first
                )
                scatter(4 + part.p, r1, part.at, part.two, part.r3, part.second)

        def step_three():
            for part in parts:
                arrived(4 + part.p, (s.size[part.second] - 1) * part.two)
                p3[q, part.kept : part.kept + part.two] = gather_sum(
                    r1, part.at, part.two, part.r3, part.second
                )
            spare = s.nz * s.z_rows - s.kept
            if spare:
                p3[q, s.kept :] = jnp.zeros((spare, C), BF16)
            for to in z_ring[1:]:
                send(6, p3.at[q, span(to * s.z_rows, s.z_rows)], r4.at[q, z], (tm, to))

        def step_four():
            arrived(6, (s.nz - 1) * s.z_rows)
            lo = span(z * s.z_rows, s.z_rows)
            total = p3[q, lo].astype(F32)
            for other in z_ring[1:]:
                total += r4[q, other].astype(F32)
            zt[q, lo] = total.astype(BF16)
            for to in z_ring[1:]:
                send(7, zt.at[q, lo], zt.at[q, lo], (tm, to))

        def chunk(part, first, second=None):
            lo = mine + part.lo + first * part.one
            return span(lo, part.one) if second is None else span(lo + second * part.two, part.two)

        def spread(i, rows, axis):
            for d in range(1, s.size[axis]):
                device = (place.lines[axis][d], z)
                send(i, out.at[rows], out.at[rows], device)

        def step_five():
            arrived(7, (s.nz - 1) * s.z_rows)
            for part in parts:
                rows = chunk(part, spot[part.first], spot[part.second])
                out[rows] = zt[q, part.kept : part.kept + part.two]
                spread(8 + part.p, rows, part.second)

        def deliver(rows):
            send(10, out.at[rows], home.at[rows], mate)

        def step_six():
            for part in parts:
                arrived(8 + part.p, (s.size[part.second] - 1) * part.two)
                rows = chunk(part, spot[part.first])
                spread(11 + part.p, rows, part.first)

        def keep():
            return pltpu.make_async_copy(
                out.at[span(mine, s.half)], home.at[span(mine, s.half)], store_sem.at[6 + q]
            )

        def step_seven():
            for part in parts:
                arrived(11 + part.p, (s.size[part.first] - 1) * part.one)
                deliver(span(mine + part.lo, part.one * s.size[part.first]))
            keep().start()

        def step_eight():
            arrived(10, s.half)
            keep().wait()

        def finish():
            sent(0, 9 * C)
            sent(1, 5 * C)
            for part in parts:
                first, second = s.size[part.first], s.size[part.second]
                sent(2 + part.p, (first - 1) * part.one)
                sent(4 + part.p, (second - 1) * part.two)
                sent(8 + part.p, (second - 1) * part.two)
                sent(11 + part.p, (first - 1) * part.one)
            sent(6, (s.nz - 1) * s.z_rows)
            sent(7, (s.nz - 1) * s.z_rows)
            sent(10, s.half)

        return [
            None,
            step_one,
            step_two,
            step_three,
            step_four,
            step_five,
            step_six,
            step_seven,
            step_eight,
            finish,
        ]

    def weight_relay(q, home, arrivals):
        out = wo.at[q]
        mate = (mate_tm, z)
        mine = core * s.half
        spot = {"y": y, "x": x}
        parts = []
        lo = at = kept = 0
        for p, (first, second, rows) in enumerate(s.parts[q]):
            part = types.SimpleNamespace(p=p, first=first, second=second, lo=lo, at=at, kept=kept)
            part.one = rows // s.size[first]
            part.two = part.one // s.size[second]
            part.ra, part.rb, part.r3 = arrivals[3 * p : 3 * p + 3]
            part.me, part.ahead, part.far, part.behind = place.rings[first]
            line = place.lines[first]
            part.to_ahead, part.to_behind = (line[1], z), (line[3], z)
            lo, at, kept = lo + rows, at + part.one, kept + part.two
            parts.append(part)

        def span(lo, rows):
            return pl.ds(pl.multiple_of(lo, 16), rows)

        def send(i, src, dst, device):
            pltpu.make_async_remote_copy(
                src_ref=src,
                dst_ref=dst,
                send_sem=w_send.at[q, i],
                recv_sem=w_recv.at[q, i],
                device_id=device,
                device_id_type=MESH,
            ).start()

        def arrived(i, rows):
            bundle(w_recv.at[q, i], wg.at[q, pl.ds(0, rows)])

        def sent(i, rows):
            bundle(w_send.at[q, i], wg.at[q, pl.ds(0, rows)])

        def scatter(i, src, lo, rows, dst, axis):
            for d in range(1, s.size[axis]):
                to = place.rings[axis][d]
                device = (place.lines[axis][d], z)
                send(i, src.at[q, span(lo + to * rows, rows)], dst.at[spot[axis]], device)

        def gather_sum(src, lo, rows, dst, axis):
            total = src[q, span(lo + spot[axis] * rows, rows)].astype(F32)
            for d in range(1, s.size[axis]):
                total += dst[place.rings[axis][d]].astype(F32)
            return total.astype(BF16)

        def step_one():
            arrived(0, 9 * C)
            arrived(1, 5 * C)

            def piece(t, carry):
                rows = span(t * C, C)
                kept = wg[q, span(mine + t * C, C)].astype(F32)
                p1[q, rows] = (kept + r1[q, rows].astype(F32)).astype(BF16)
                return carry

            for part in parts:
                lax.fori_loop(part.lo // C, (part.lo + 4 * part.one) // C, piece, 0)
                half = part.one // 2
                lo = part.lo + part.far * part.one
                send(2 + part.p, p1.at[q, span(lo, half)], part.ra.at[0], part.to_ahead)
                send(2 + part.p, p1.at[q, span(lo + half, half)], part.ra.at[1], part.to_behind)

        def step_two():
            for part in parts:
                half = part.one // 2
                arrived(2 + part.p, part.one)
                for side, to, skip in ((0, part.ahead, 0), (1, part.behind, half)):
                    rows = span(part.lo + to * part.one + skip, half)
                    total = p1[q, rows].astype(F32) + part.ra[side].astype(F32)
                    p1[q, rows] = total.astype(BF16)
                for side, to, device in (
                    (0, part.ahead, part.to_ahead),
                    (1, part.behind, part.to_behind),
                ):
                    rows = span(part.lo + to * part.one, part.one)
                    send(4 + part.p, p1.at[q, rows], part.rb.at[side], device)

        def step_three():
            for part in parts:
                arrived(4 + part.p, 2 * part.one)
                total = p1[q, span(part.lo + part.me * part.one, part.one)].astype(F32)
                total += part.rb[0].astype(F32) + part.rb[1].astype(F32)
                r1[q, part.at : part.at + part.one] = total.astype(BF16)
                scatter(6 + part.p, r1, part.at, part.two, part.r3, part.second)

        def step_reduced():
            for part in parts:
                arrived(6 + part.p, (s.size[part.second] - 1) * part.two)
                p3[q, part.kept : part.kept + part.two] = gather_sum(
                    r1, part.at, part.two, part.r3, part.second
                )
            spare = s.nz * s.z_rows - s.kept
            if spare:
                p3[q, s.kept :] = jnp.zeros((spare, C), BF16)
            for to in z_ring[1:]:
                send(8, p3.at[q, span(to * s.z_rows, s.z_rows)], r4.at[q, z], (tm, to))

        def step_four():
            arrived(8, (s.nz - 1) * s.z_rows)
            lo = span(z * s.z_rows, s.z_rows)
            total = p3[q, lo].astype(F32)
            for other in z_ring[1:]:
                total += r4[q, other].astype(F32)
            zt[q, lo] = total.astype(BF16)
            for to in z_ring[1:]:
                send(9, zt.at[q, lo], zt.at[q, lo], (tm, to))

        def chunk(part, first, skip=0, rows=None):
            return span(mine + part.lo + first * part.one + skip, part.one if rows is None else rows)

        def step_five():
            arrived(9, (s.nz - 1) * s.z_rows)
            for part in parts:
                rows = chunk(part, part.me, spot[part.second] * part.two, part.two)
                out[rows] = zt[q, part.kept : part.kept + part.two]
                for d in range(1, s.size[part.second]):
                    device = (place.lines[part.second][d], z)
                    send(10 + part.p, out.at[rows], out.at[rows], device)

        def deliver(rows):
            send(16, out.at[rows], home.at[rows], mate)

        def step_six():
            for part in parts:
                arrived(10 + part.p, (s.size[part.second] - 1) * part.two)
                rows = chunk(part, part.me)
                send(12 + part.p, out.at[rows], out.at[rows], part.to_ahead)
                send(12 + part.p, out.at[rows], out.at[rows], part.to_behind)
        def step_seven():
            for part in parts:
                half = part.one // 2
                arrived(12 + part.p, 2 * part.one)
                rows = chunk(part, part.behind, 0, half)
                send(14 + part.p, out.at[rows], out.at[rows], part.to_ahead)
                rows = chunk(part, part.ahead, half, half)
                send(14 + part.p, out.at[rows], out.at[rows], part.to_behind)
        def keep():
            return pltpu.make_async_copy(
                out.at[span(mine, s.half)], home.at[span(mine, s.half)], store_sem.at[6 + q]
            )

        def step_eight():
            for part in parts:
                arrived(14 + part.p, part.one)
            deliver(span(mine, s.half))
            keep().start()

        def step_nine():
            arrived(16, s.half)
            keep().wait()

        def finish():
            sent(0, 9 * C)
            sent(1, 5 * C)
            for part in parts:
                sent(2 + part.p, part.one)
                sent(4 + part.p, 2 * part.one)
                sent(6 + part.p, (s.size[part.second] - 1) * part.two)
                sent(10 + part.p, (s.size[part.second] - 1) * part.two)
                sent(12 + part.p, 2 * part.one)
                sent(14 + part.p, part.one)
            sent(8, (s.nz - 1) * s.z_rows)
            sent(9, (s.nz - 1) * s.z_rows)
            sent(16, s.half)

        return [
            None,
            step_one,
            step_two,
            step_three,
            step_reduced,
            step_four,
            step_five,
            step_six,
            step_seven,
            step_eight,
            step_nine,
            finish,
        ]

    def store(i, src, dst):
        copy = pltpu.make_async_copy(src, dst, store_sem.at[i])
        copy.start()
        return copy

    loads[0].wait()
    payload = place.local_stats(place.own(x_ref))
    place.meet()
    place.ar_start(0, 0, payload)
    place.halo_start(0, xe, True)
    loads[1].wait()
    place.halo_start(1, ue, False)
    for load in loads[2:]:
        load.wait()
    gain1, shift1, gain2, shift2 = (vectors[i] for i in range(4))
    turn(w2_ref, wf2)
    place.stats_stage(0, 0)
    turn(w1_ref, wf1)
    place.halo_wait(0, xe)
    copy_first(place, xe)
    stats1 = place.stats_stage(0, 1)

    build_act(xe, a1, stats1, gain1, shift1)
    for f, value in enumerate(conv(a1, taps_of(w1_ref))):
        he[2 + f, 1 : R + 1] = value.astype(BF16).reshape(R, W, C)
    hidden = place.own_block(he, 2)
    place.ar_start(1, 0, place.local_stats(place.own(hidden)))
    place.halo_wait(1, ue)
    blank_next(place, ue)
    build_grad(ue)
    place.stats_stage(1, 0)
    place.halo_start(2, he, True)
    back_conv(g3, wf2)
    back_first(g3, wf2)
    place.halo_wait(2, he)
    copy_first(place, he)
    stats2 = place.stats_stage(1, 1)

    second = weight_relay(1, wo2_hbm, arrivals[4:])
    first = weight_reduce(0, wo1_hbm, arrivals[:4])
    place.ar_start(2, 0, norm_back_sums(hidden, stats2, gain2, shift2))
    build_act(he, a2, stats2, gain2, shift2)
    place.sums_stage(2, 0)
    weight_grad(a2, u_ref, 1)
    sums2 = place.sums_stage(2, 1)
    for f in range(F):
        value = norm_back_value(hidden, stats2, gain2, sums2, f)
        ge[f, 1 : R + 1] = value.astype(BF16).reshape(R, W, C)
    place.halo_start(3, ge, False)
    second[1]()
    weight_grad(a1, place.own_block(ge, 0), 0)
    second[2]()
    first[1]()
    place.halo_wait(3, ge)
    blank_next(place, ge)
    build_grad(ge)
    second[3]()
    back_conv(g3, wf1)
    back_first(g3, wf1)
    place.ar_start(3, 0, norm_back_sums(x_ref, stats1, gain1, shift1))
    first[2]()
    second[4]()
    branch = conv(a2, taps_of(w2_ref))
    for f in range(F):
        total = x_ref[f].astype(F32).reshape(cells, C) + branch[f]
        out_ref[f] = total.astype(BF16).reshape(R, W, C)
    stores = [store(0, out_ref, out_hbm)]
    first[3]()
    place.sums_stage(3, 0)
    second[5]()
    first[4]()
    second[6]()
    sums1 = place.sums_stage(3, 1)
    first[5]()
    second[7]()
    for f in range(F):
        value = norm_back_value(x_ref, stats1, gain1, sums1, f)
        total = u_ref[f].astype(F32).reshape(cells, C) + value
        ig_ref[f] = total.astype(BF16).reshape(R, W, C)
    stores.append(store(1, ig_ref, ig_hbm))
    first[6]()
    second[8]()
    for i, (row, result) in enumerate(zip(sums1 + sums2, (gg1_hbm, sg1_hbm, gg2_hbm, sg2_hbm))):
        results[i] = row
        stores.append(store(2 + i, results.at[i], result))
    second[9]()
    first[7]()
    second[10]()
    first[8]()

    for copy in stores:
        copy.wait()
    second[11]()
    first[9]()
    for k in range(4):
        place.ar_sent(k)
    for q, ref in enumerate((xe, ue, he, ge)):
        place.halo_sent(q, ref)


def finish_kernel(*refs):
    sources, places, (fields, vectors, narrow, wide, load_sem, sem) = refs[:8], refs[8:16], refs[16:]
    copies = []

    def load(i, src, dst):
        copy = pltpu.make_async_copy(src, dst, load_sem.at[i])
        copy.start()
        return copy

    def write(src, dst):
        copy = pltpu.make_async_copy(src, dst, sem.at[len(copies)])
        copy.start()
        copies.append(copy)

    spans = ((0, 9), (9, 10), (19, 9))
    weights = []
    for j, (lo, count) in enumerate(spans):
        for q in range(2):
            rows = pl.ds(lo * C, count * C)
            weights.append(load(2 * j + q, sources[2 + q].at[rows], narrow.at[q, rows]))
    bounce = [(i, fields.at[i]) for i in range(2)] + [(4 + i, vectors.at[i]) for i in range(4)]
    others = [load(6 + n, sources[i], ref) for n, (i, ref) in enumerate(bounce)]
    for j, (lo, count) in enumerate(spans):
        for q in range(2):
            weights[2 * j + q].wait()
            for i in range(3):
                to = (9 * i + 3 * j) * C
                for k in range(3):
                    at = 3 * i + k
                    tap = lo + at + (1 if count == 10 and at >= 5 else 0)
                    block = narrow[q, tap * C : (tap + 1) * C]
                    wide[q, to + k * C : to + (k + 1) * C] = block.astype(F32)
                rows = pl.ds(to, 3 * C)
                write(wide.at[q, rows], places[2 + q].at[rows])
        if j == 0:
            for copy, (i, ref) in zip(others, bounce):
                copy.wait()
                write(ref, places[i])
    for copy in copies:
        copy.wait()


def body(inputs, gain1, shift1, weight1, gain2, shift2, weight2, upstream):
    F, R, W, _ = inputs.shape
    s = plan_of(lax.axis_size("tm"), lax.axis_size("height"), F, R, W)
    E, RE = F + 2, R + 2
    cells = R * W
    hbm = pl.BlockSpec(memory_space=pltpu.HBM)
    field = jax.ShapeDtypeStruct(inputs.shape, BF16)
    weights = jax.ShapeDtypeStruct((s.taps * C, C), BF16)
    vector = jax.ShapeDtypeStruct((1, C), F32)
    wide = pltpu.VMEM((E, RE, W, C), BF16)
    wider = pltpu.VMEM((E, RE, W, 3 * C), BF16)
    arrivals = []
    for first, second, rows in s.parts[0]:
        one = rows // s.size[first]
        arrivals.append(pltpu.VMEM((s.size[first], one, C), BF16))
        arrivals.append(pltpu.VMEM((s.size[second], one // s.size[second], C), BF16))
    for first, second, rows in s.parts[1]:
        one = rows // s.size[first]
        arrivals.append(pltpu.VMEM((2, one // 2, C), BF16))
        arrivals.append(pltpu.VMEM((2, one, C), BF16))
        arrivals.append(pltpu.VMEM((s.size[second], one // s.size[second], C), BF16))
    room = 60 * 1024 * 1024
    results = pl.pallas_call(
        functools.partial(kernel, s),
        out_shape=[field, field, weights, weights, vector, vector, vector, vector],
        in_specs=[hbm] * 8,
        out_specs=[hbm] * 8,
        scratch_shapes=[
            pltpu.VMEM((27, C, C), BF16),
            pltpu.VMEM((27, C, C), BF16),
            pltpu.VMEM((3, 9 * C, C), BF16),
            pltpu.VMEM((3, 9 * C, C), BF16),
            pltpu.VMEM((4, 1, C), F32),
            pltpu.VMEM((F, R, W, C), BF16),
            pltpu.VMEM((F, R, W, C), BF16),
            pltpu.VMEM((2, s.taps * C, C), BF16),
            pltpu.VMEM((4, 1, C), F32),
            wide,
            wide,
            wide,
            wide,
            wider,
            wider,
            wider,
            pltpu.VMEM((F, cells, C), F32),
            pltpu.VMEM((F, cells, C), F32),
            pltpu.VMEM((8, max(s.stages), 2, C), F32),
            pltpu.VMEM((2, s.taps * C, C), BF16),
            pltpu.VMEM((2, s.half, C), BF16),
            pltpu.VMEM((2, s.half, C), BF16),
            pltpu.VMEM((2, s.nz * s.z_rows, C), BF16),
            pltpu.VMEM((2, s.nz, s.z_rows, C), BF16),
            pltpu.VMEM((2, s.nz * s.z_rows, C), BF16),
            arrivals,
            pltpu.SemaphoreType.DMA((8,)),
            pltpu.SemaphoreType.DMA((8,)),
            pltpu.SemaphoreType.DMA((4,)),
            pltpu.SemaphoreType.DMA((4,)),
            pltpu.SemaphoreType.DMA((2, 17)),
            pltpu.SemaphoreType.DMA((2, 17)),
            pltpu.SemaphoreType.DMA((8,)),
            pltpu.SemaphoreType.DMA((8,)),
        ],
        compiler_params=pltpu.CompilerParams(
            collective_id=0, has_side_effects=True, vmem_limit_bytes=room
        ),
        cost_estimate=pl.CostEstimate(
            flops=6 * 2 * F * cells * 27 * C * C, bytes_accessed=8_000_000, transcendentals=1_000_000
        ),
    )(
        inputs,
        upstream,
        weight1.reshape(27, C, C),
        weight2.reshape(27, C, C),
        gain1.reshape(1, C),
        shift1.reshape(1, C),
        gain2.reshape(1, C),
        shift2.reshape(1, C),
    )
    total = jax.ShapeDtypeStruct((27 * C, C), F32)
    output, input_grad, first, second, gg1, sg1, gg2, sg2 = pl.pallas_call(
        finish_kernel,
        out_shape=[field, field, total, total, vector, vector, vector, vector],
        in_specs=[hbm] * 8,
        out_specs=[hbm] * 8,
        scratch_shapes=[
            pltpu.VMEM((2, F, R, W, C), BF16),
            pltpu.VMEM((4, 1, C), F32),
            pltpu.VMEM((2, s.taps * C, C), BF16),
            pltpu.VMEM((2, 27 * C, C), F32),
            pltpu.SemaphoreType.DMA((12,)),
            pltpu.SemaphoreType.DMA((24,)),
        ],
        compiler_params=pltpu.CompilerParams(vmem_limit_bytes=room),
        cost_estimate=pl.CostEstimate(flops=0, bytes_accessed=6_000_000, transcendentals=0),
    )(*results)
    return (
        output,
        input_grad,
        first.reshape(3, 3, 3, C, C),
        second.reshape(3, 3, 3, C, C),
        gg1.reshape(C),
        sg1.reshape(C),
        gg2.reshape(C),
        sg2.reshape(C),
    )


def solution(mesh):
    fields = P("tm", "height", None, None)
    return jax.shard_map(
        body,
        mesh=mesh,
        in_specs=(fields, P(), P(), P(), P(), P(), P(), fields),
        out_specs=(fields, fields, P(), P(), P(), P(), P(), P()),
        check_vma=False,
    )
```

```python
import functools
import types

import jax
import jax.numpy as jnp
from jax import lax
from jax.experimental import pallas as pl
from jax.experimental.pallas import tpu as pltpu
from jax.sharding import PartitionSpec as P

C = 128
G = 32
MEMBERS = C // G
EPSILON = 1e-06
MESH = pl.DeviceIdType.MESH
F32 = jnp.float32
BF16 = jnp.bfloat16


def plan_of(tm, height, frames, rows, columns):
    s = types.SimpleNamespace()
    s.tm, s.nz = tm, height
    s.nyx = tm // 2
    s.nx = 4 if s.nyx >= 16 else 2
    s.ny = s.nyx // s.nx
    s.frames, s.rows, s.columns = frames, rows, columns
    s.stages = (2 * s.nz, s.nyx)
    s.taps = 28
    s.half = s.taps * C // 2
    most = min(s.nz - 1, 7) if s.nz > 2 else 2
    s.parts = (
        (("x", "y", 1024, 0, s.nz // 2), ("y", "x", s.half - 1024, s.nz // 2, most - s.nz // 2)),
        (("y", "x", s.half, 0, most),),
    )
    s.size = {"y": s.ny, "x": s.nx}
    s.tile = max(
        rows // s.size[first] // (s.size[second] * count)
        for parts in s.parts
        for first, second, rows, _, count in parts
    )
    return s


def bundle(sem, ref):
    pltpu.make_async_copy(ref, ref, sem).wait()


def group_total(row):
    lane = lax.broadcasted_iota(jnp.int32, row.shape, 1)
    for step in (1, 2):
        ahead = pltpu.roll(row, C - step, 1)
        behind = pltpu.roll(row, step, 1)
        row = row + jnp.where(lane & step == 0, ahead, behind)
    return row


def wrap(i, n):
    return jnp.where(i >= n, i - n, i)


def sigmoid(u):
    return 1.0 / (1.0 + jnp.exp(-u))


class Place:
    def __init__(self, s):
        self.s = s
        self.tm = tm = lax.axis_index("tm")
        self.z = z = lax.axis_index("height")
        self.core = core = tm % 2
        self.yx = yx = tm // 2
        self.x = yx % s.nx
        self.y = yx // s.nx
        self.mate_tm = mate_tm = tm + 1 - 2 * core
        self.z_ring = z_ring = [z] + [wrap(z + d, s.nz) for d in range(1, s.nz)]
        self.x_ring = [self.x] + [wrap(self.x + d, s.nx) for d in range(1, s.nx)]
        self.y_ring = [self.y] + [wrap(self.y + d, s.ny) for d in range(1, s.ny)]
        self.rings = {"y": self.y_ring, "x": self.x_ring}
        self.row = [self.tm_of(self.y, q, core) for q in self.x_ring]
        self.column = [self.tm_of(q, self.x, core) for q in self.y_ring]
        self.lines = {"y": self.column, "x": self.row}
        self.groups = (
            (core * s.nz + z, [(tm, q) for q in z_ring[1:]] + [(mate_tm, q) for q in z_ring]),
            (yx, [(wrap(yx + d, s.nyx) * 2 + core, z) for d in range(1, s.nyx)]),
        )
        self.tm_next, self.tm_prev = wrap(tm + 1, s.tm), wrap(tm + s.tm - 1, s.tm)
        self.z_next, self.z_prev = z_ring[1], z_ring[-1]
        self.partners = [peer for _, peers in self.groups for peer in peers]
        self.partners = self.partners + [
            (t, q) for t in (self.tm_next, self.tm_prev) for q in (z, self.z_next, self.z_prev)
        ]
        self.partners = self.partners + [
            (t, q) for line in (self.row, self.column) for t in line[1:] for q in z_ring[1:]
        ]

    def tm_of(self, y, x, core):
        return (y * self.s.nx + x) * 2 + core

    def greet(self):
        barrier = pltpu.get_barrier_semaphore()
        for partner in self.partners:
            pl.semaphore_signal(barrier, inc=1, device_id=partner, device_id_type=MESH)

    def meet(self):
        pl.semaphore_wait(pltpu.get_barrier_semaphore(), len(self.partners))

    def own_block(self, ref, lo):
        return ref.at[pl.ds(lo, self.s.frames), pl.ds(1, self.s.rows)]

    def own(self, ref):
        return ref[...].astype(F32).reshape(-1, C)

    def bind(self, ar, ar_send, ar_recv, halo_send, halo_recv):
        self.ar, self.ar_send, self.ar_recv = ar, ar_send, ar_recv
        self.halo_send, self.halo_recv = halo_send, halo_recv

    def ar_start(self, k, stage, payload):
        i = 2 * k + stage
        slot, peers = self.groups[stage]
        self.ar[i, slot, 0:1] = payload[0]
        self.ar[i, slot, 1:2] = payload[1]
        for peer in peers:
            pltpu.make_async_remote_copy(
                src_ref=self.ar.at[i, slot],
                dst_ref=self.ar.at[i, slot],
                send_sem=self.ar_send.at[i],
                recv_sem=self.ar_recv.at[i],
                device_id=peer,
                device_id_type=MESH,
            ).start()

    def ar_wait(self, k, stage):
        i = 2 * k + stage
        n = self.s.stages[stage]
        bundle(self.ar_recv.at[i], self.ar.at[i, pl.ds(0, n - 1)])
        parts = [self.ar[i, j] for j in range(n)]
        return [p[0:1] for p in parts], [p[1:2] for p in parts]

    def ar_sent(self, k):
        for stage, n in enumerate(self.s.stages):
            i = 2 * k + stage
            bundle(self.ar_send.at[i], self.ar.at[i, pl.ds(0, n - 1)])

    def local_count(self):
        return float(self.s.frames * self.s.rows * self.s.columns * MEMBERS)

    def local_stats(self, v):
        centre = group_total(jnp.sum(v, axis=0, keepdims=True)) / self.local_count()
        spread = group_total(jnp.sum((v - centre) ** 2, axis=0, keepdims=True))
        return centre, spread

    def join_stats(self, parts, count):
        means, spreads = parts
        centre = sum(means) / float(len(means))
        spread = sum(spreads) + count * sum((mean - centre) ** 2 for mean in means)
        return centre, spread

    def stats_stage(self, k, stage):
        count = self.local_count()
        for n in self.s.stages[:stage]:
            count = count * n
        joined = self.join_stats(self.ar_wait(k, stage), count)
        if stage < 1:
            return self.ar_start(k, stage + 1, joined)
        centre, spread = joined
        return centre, lax.rsqrt(spread / (count * self.s.stages[stage]) + EPSILON)

    def sums_stage(self, k, stage):
        first, second = self.ar_wait(k, stage)
        totals = sum(first), sum(second)
        return totals if stage == 1 else self.ar_start(k, stage + 1, totals)

    def halo_start(self, q, ref, ahead):
        F, R, z = self.s.frames, self.s.rows, self.z
        target = self.tm_next if ahead else self.tm_prev
        far, near = (0, 2) if ahead else (2, 0)
        frames = pl.ds(near, F)
        everything = ref.at[frames, pl.ds(1, R)]
        top, bottom = ref.at[frames, pl.ds(1, 1)], ref.at[frames, pl.ds(R, 1)]
        copies = [
            (everything, ref.at[pl.ds(far, F), pl.ds(1, R)], (target, z)),
            (top, ref.at[pl.ds(near, F), pl.ds(R + 1, 1)], (self.tm, self.z_prev)),
            (bottom, ref.at[pl.ds(near, F), pl.ds(0, 1)], (self.tm, self.z_next)),
            (top, ref.at[pl.ds(far, F), pl.ds(R + 1, 1)], (target, self.z_prev)),
            (bottom, ref.at[pl.ds(far, F), pl.ds(0, 1)], (target, self.z_next)),
        ]
        for piece, place, device in copies:
            pltpu.make_async_remote_copy(
                src_ref=piece,
                dst_ref=place,
                send_sem=self.halo_send.at[q],
                recv_sem=self.halo_recv.at[q],
                device_id=device,
                device_id_type=MESH,
            ).start()

    def halo_bytes(self, sem, ref):
        F, R = self.s.frames, self.s.rows
        bundle(sem, ref.at[pl.ds(0, F + 2), pl.ds(0, F * (R + 4) // (F + 2))])

    def halo_wait(self, q, ref):
        self.halo_bytes(self.halo_recv.at[q], ref)

    def halo_sent(self, q, ref):
        self.halo_bytes(self.halo_send.at[q], ref)


def blank_next(place, ref):
    F = place.s.frames

    @pl.when(place.tm == place.s.tm - 1)
    def _():
        ref[F : F + 2] = jnp.zeros((2,) + ref.shape[1:], ref.dtype)


def copy_first(place, ref):
    @pl.when(place.tm == 0)
    def _():
        ref[0] = ref[2]
        ref[1] = ref[2]


def kernel(
    s,
    x_hbm,
    u_hbm,
    w1_hbm,
    w2_hbm,
    g1_hbm,
    s1_hbm,
    g2_hbm,
    s2_hbm,
    out_hbm,
    ig_hbm,
    wo1_hbm,
    wo2_hbm,
    gg1_hbm,
    sg1_hbm,
    gg2_hbm,
    sg2_hbm,
    w1_ref,
    w2_ref,
    wf1,
    wf2,
    vectors,
    out_ref,
    ig_ref,
    wo,
    results,
    xe,
    ue,
    he,
    ge,
    a1,
    a2,
    g3,
    dact,
    pre_buf,
    ar,
    wg,
    r1,
    p1,
    rx,
    arrivals,
    ar_send,
    ar_recv,
    halo_send,
    halo_recv,
    w_send,
    w_recv,
    load_sem,
    store_sem,
):
    F, R, W = s.frames, s.rows, s.columns
    E, RE = F + 2, R + 2
    cells = R * W
    place = Place(s)
    place.bind(ar, ar_send, ar_recv, halo_send, halo_recv)
    tm, z, x, y, core = place.tm, place.z, place.x, place.y, place.core
    mate_tm, z_ring = place.mate_tm, place.z_ring

    x_ref, u_ref = place.own_block(xe, 2), place.own_block(ue, 0)
    loads = [
        (x_hbm, x_ref),
        (u_hbm, u_ref),
        (w1_hbm, w1_ref),
        (w2_hbm, w2_ref),
        (g1_hbm, vectors.at[0]),
        (s1_hbm, vectors.at[1]),
        (g2_hbm, vectors.at[2]),
        (s2_hbm, vectors.at[3]),
    ]
    loads = [pltpu.make_async_copy(a, b, load_sem.at[i]) for i, (a, b) in enumerate(loads)]
    for load in loads:
        load.start()
    place.greet()

    def shifted(v, dst, f):
        column = lax.broadcasted_iota(jnp.int32, v.shape, 0) & (W - 1)
        left = jnp.where(column == 0, 0.0, pltpu.roll(v, 1, 0))
        right = jnp.where(column == W - 1, 0.0, pltpu.roll(v, RE * W - 1, 0))
        for k, piece in enumerate((left, v, right)):
            dst[f, :, :, k * C : (k + 1) * C] = piece.astype(BF16).reshape(RE, W, C)

    def blank_rows(dst):
        blank = jnp.zeros((E, 1) + dst.shape[2:], dst.dtype)

        @pl.when(z == 0)
        def _():
            dst[:, 0:1] = blank

        @pl.when(z == s.nz - 1)
        def _():
            dst[:, R + 1 : R + 2] = blank

    def build_act(src, dst, stats, gain, shift):
        centre, inverse = stats
        scale = inverse * gain

        def frame(f, carry):
            v = src[f].astype(F32).reshape(RE * W, C)
            affine = (v - centre) * scale + shift
            shifted(affine * sigmoid(affine), dst, f)
            return carry

        lax.fori_loop(0, E, frame, 0)
        blank_rows(dst)

    def build_grad(src):
        def frame(f, carry):
            shifted(src[f].astype(F32).reshape(RE * W, C), g3, f)
            return carry

        lax.fori_loop(0, E, frame, 0)
        blank_rows(g3)

    def dot(a, b):
        return jnp.dot(a, b, preferred_element_type=F32)

    def turn(src, dst):
        for at in range(27):
            dst[at // 9, (at % 9) * C : (at % 9 + 1) * C, :] = src[26 - at].T

    def patches(src, f):
        return jnp.concatenate([src[f, j : j + R].reshape(cells, 3 * C) for j in range(3)], axis=1)

    def conv(src, taps):
        first = dot(patches(src, 0), taps[0])
        second = None
        for f in (1, 2):
            both = dot(patches(src, f), jnp.concatenate([taps[f], taps[f - 1]], axis=1))
            first = first + both[:, :C]
            second = both[:, C:] if second is None else second + both[:, C:]
        return first, second + dot(patches(src, 3), taps[2])

    def taps_of(weight):
        return [weight[9 * i : 9 * i + 9].reshape(9 * C, C) for i in range(3)]

    def back_conv(src, weight):
        dact[0], dact[1] = conv(src, [weight[i] for i in range(3)])

    def back_first(src, weight):
        @pl.when(tm == 0)
        def _():
            both = dot(patches(src, 0), jnp.concatenate([weight[1], weight[2]], axis=1))
            dact[0] += both[:, :C] + both[:, C:] + dot(patches(src, 1), weight[2])

    def weight_grad(act, grad, q):
        turned = [grad[f].reshape(cells, C).T for f in range(F)]
        both = jnp.concatenate(turned, axis=0)
        wg[q, 14 * C : 15 * C, :] = jnp.zeros((C, C), BF16)
        mate = (mate_tm, z)

        def row_tap(j, base):
            window = [act[f, pl.ds(j, R)].reshape(cells, 3 * C) for f in range(E)]
            one, two = dot(both, window[1]), dot(both, window[2])
            sums = (
                dot(turned[0], window[0]) + one[C:],
                one[:C] + two[C:],
                two[:C] + dot(turned[1], window[3]),
            )
            for i, total in enumerate(sums):
                total = total.astype(BF16)
                for k in range(3):
                    at = 3 * i + k
                    lo = base(at) * C
                    wg[q, pl.ds(pl.multiple_of(lo, C), C), :] = total[:, k * C : (k + 1) * C].T

        def send(i, src, dst, taps):
            pltpu.make_async_remote_copy(
                src_ref=wg.at[q, pl.ds(pl.multiple_of(src * C, C), taps * C)],
                dst_ref=r1.at[q, pl.ds(pl.multiple_of(dst * C, C), taps * C)],
                send_sem=w_send.at[q, i],
                recv_sem=w_recv.at[q, i],
                device_id=mate,
                device_id_type=MESH,
            ).start()

        row_tap(2 - 2 * core, lambda at: (1 - core) * 19 + at)
        send(0, (1 - core) * 19, (1 - core) * 5, 9)
        row_tap(1, lambda at: 9 + at if at < 5 else 10 + at)
        send(1, 14 - core * 5, core * 9, 5)
        row_tap(2 * core, lambda at: core * 19 + at)

    def norm_back_sums(values, stats, gain, shift):
        centre, inverse = stats
        total_cross = jnp.zeros((1, C), F32)
        total = jnp.zeros((1, C), F32)
        for f in range(F):
            normed = (values[f].astype(F32).reshape(cells, C) - centre) * inverse
            affine = normed * gain + shift
            sig = sigmoid(affine)
            pre = dact[f] * sig * (1.0 + affine * (1.0 - sig))
            pre_buf[f] = pre
            total_cross += jnp.sum(pre * normed, axis=0, keepdims=True)
            total += jnp.sum(pre, axis=0, keepdims=True)
        return total_cross, total

    def norm_back_value(values, stats, gain, sums, f):
        centre, inverse = stats
        gain_grad, shift_grad = sums
        members = float(F * cells * MEMBERS * s.tm * s.nz)
        mean_grad = group_total(gain * shift_grad) / members
        mean_cross = group_total(gain * gain_grad) / members
        normed = (values[f].astype(F32).reshape(cells, C) - centre) * inverse
        return inverse * (pre_buf[f] * gain - mean_grad - normed * mean_cross)

    def weight_sum(q, home, arrivals, relay):
        out = wo.at[q]
        mate = (mate_tm, z)
        mine = core * s.half
        spot = {"y": y, "x": x}
        parts = []
        lo = at = 0
        for p, (first, second, rows, z_lo, z_count) in enumerate(s.parts[q]):
            part = types.SimpleNamespace(p=p, first=first, second=second, lo=lo, at=at, z_lo=z_lo)
            part.zs = range(z_lo, z_lo + z_count)
            part.n = s.size[first]
            part.one = rows // part.n
            part.tile = part.one // (s.size[second] * z_count)
            part.ring, part.line = place.rings[first], place.lines[first]
            part.owner = jnp.logical_and(z >= z_lo, z < z_lo + z_count)
            part.slot = z * s.size[second] + spot[second]
            part.own = ((z - z_lo) * s.size[second] + spot[second]) * part.tile
            lo, at = lo + rows, at + part.one
            parts.append(part)
        plane = s.nz * 4

        def span(lo, rows):
            return pl.ds(pl.multiple_of(lo, 16), rows)

        def send(i, src, dst, device, arrival=None):
            pltpu.make_async_remote_copy(
                src_ref=src,
                dst_ref=dst,
                send_sem=w_send.at[q, i],
                recv_sem=w_recv.at[q, i if arrival is None else arrival],
                device_id=device,
                device_id_type=MESH,
            ).start()

        def arrived(i, rows):
            bundle(w_recv.at[q, i], wg.at[q, pl.ds(0, rows)])

        def sent(i, rows):
            bundle(w_send.at[q, i], wg.at[q, pl.ds(0, rows)])

        def add_mate(part):
            def piece(t, carry):
                rows = span(t * C, C)
                kept = wg[q, span(mine + t * C, C)].astype(F32)
                p1[q, rows] = (kept + r1[q, rows].astype(F32)).astype(BF16)
                return carry

            lax.fori_loop(part.lo // C, (part.lo + part.n * part.one) // C, piece, 0)

        def rows_of(part, i, skip=0, rows=None):
            return span(part.lo + i * part.one + skip, part.one if rows is None else rows)

        def step_mate():
            arrived(0, 9 * C)
            arrived(1, 5 * C)
            for part in parts:
                add_mate(part)
                if relay:
                    half = part.one // 2
                    far = part.ring[2]
                    one = p1.at[q, rows_of(part, far, 0, half)]
                    two = p1.at[q, rows_of(part, far, half, half)]
                    send(2, one, arrivals[0].at[0], (part.line[1], z))
                    send(2, two, arrivals[0].at[1], (part.line[3], z))
                else:
                    for d in range(1, part.n):
                        src = p1.at[q, rows_of(part, part.ring[d])]
                        dst = arrivals[part.p].at[part.ring[0]]
                        send(2 + part.p, src, dst, (part.line[d], z))

        def step_relay():
            (part,) = parts
            half = part.one // 2
            arrived(2, part.one)
            for side, to, skip in ((0, 1, 0), (1, 3, half)):
                rows = rows_of(part, part.ring[to], skip, half)
                total = p1[q, rows].astype(F32) + arrivals[0][side].astype(F32)
                p1[q, rows] = total.astype(BF16)
            for side, to in ((0, 1), (1, 3)):
                src = p1.at[q, rows_of(part, part.ring[to])]
                send(3, src, arrivals[1].at[side], (part.line[to], z))

        def step_plane():
            for part in parts:
                total = p1[q, rows_of(part, part.ring[0])].astype(F32)
                if relay:
                    arrived(3, 2 * part.one)
                    total += arrivals[1][0].astype(F32) + arrivals[1][1].astype(F32)
                else:
                    arrived(2 + part.p, (part.n - 1) * part.one)
                    for d in range(1, part.n):
                        total += arrivals[part.p][part.ring[d]].astype(F32)
                r1[q, part.at : part.at + part.one] = total.astype(BF16)
                across, line = place.rings[part.second], place.lines[part.second]
                for d in range(s.size[part.second]):
                    for owner_z in part.zs:

                        def go(part=part, d=d, owner_z=owner_z, across=across, line=line):
                            tile = (owner_z - part.z_lo) * s.size[part.second] + across[d]
                            src = r1.at[q, span(part.at + tile * part.tile, part.tile)]
                            dst = rx.at[q, part.slot, pl.ds(0, part.tile)]
                            send(4 + part.p, src, dst, (line[d], owner_z), 4)

                        if d:
                            go()
                        else:
                            pl.when(z != owner_z)(go)

        def step_own():
            for part in parts:

                @pl.when(part.owner)
                def _(part=part):
                    arrived(4, (plane - 1) * part.tile)
                    tile = pl.ds(0, part.tile)
                    rx[q, part.slot, tile] = r1[q, span(part.at + part.own, part.tile)]
                    total = rx[q, 0, tile].astype(F32)
                    for j in range(1, plane):
                        total += rx[q, j, tile].astype(F32)
                    lo = mine + part.lo + part.ring[0] * part.one + part.own
                    rows = span(lo, part.tile)
                    out[rows] = total.astype(BF16)
                    for t, column in enumerate(place.lines[part.second]):
                        for d, other in enumerate(z_ring):
                            if t or d:
                                send(6 + part.p, out.at[rows], out.at[rows], (column, other))

        def chunk(part, i, skip=0, rows=None):
            return span(mine + part.lo + i * part.one + skip, part.one if rows is None else rows)

        def step_ring():
            for part in parts:

                @pl.when(part.owner)
                def _(part=part):
                    arrived(6 + part.p, part.one - part.tile)

                @pl.when(jnp.logical_not(part.owner))
                def _(part=part):
                    arrived(6 + part.p, part.one)

                rows = chunk(part, part.ring[0])
                for d in (1, 3) if relay else range(1, part.n):
                    send(8 + part.p, out.at[rows], out.at[rows], (part.line[d], z))

        def step_relay_back():
            (part,) = parts
            half = part.one // 2
            arrived(8, 2 * part.one)
            rows = chunk(part, part.ring[3], 0, half)
            send(9, out.at[rows], out.at[rows], (part.line[1], z))
            rows = chunk(part, part.ring[1], half, half)
            send(9, out.at[rows], out.at[rows], (part.line[3], z))

        def keep():
            return pltpu.make_async_copy(
                out.at[span(mine, s.half)], home.at[span(mine, s.half)], store_sem.at[6 + q]
            )

        def step_deliver():
            for part in parts:
                if relay:
                    arrived(9, part.one)
                else:
                    arrived(8 + part.p, (part.n - 1) * part.one)
                rows = span(mine + part.lo, part.n * part.one)
                send(16, out.at[rows], home.at[rows], mate)
            keep().start()

        def step_end():
            arrived(16, s.half)
            keep().wait()

        def finish():
            sent(0, 9 * C)
            sent(1, 5 * C)
            sent(16, s.half)
            for part in parts:
                if relay:
                    sent(2, part.one)
                    sent(3, 2 * part.one)
                    sent(8, 2 * part.one)
                    sent(9, part.one)
                else:
                    sent(2 + part.p, (part.n - 1) * part.one)
                    sent(8 + part.p, (part.n - 1) * part.one)

                @pl.when(part.owner)
                def _(part=part):
                    sent(4 + part.p, part.one - part.tile)
                    sent(6 + part.p, (plane - 1) * part.tile)

                @pl.when(jnp.logical_not(part.owner))
                def _(part=part):
                    sent(4 + part.p, part.one)

        if relay:
            steps = [step_mate, step_relay, step_plane, step_own, step_ring, step_relay_back]
        else:
            steps = [step_mate, step_plane, step_own, step_ring]
        return steps + [step_deliver, step_end, finish]

    def store(i, src, dst):
        copy = pltpu.make_async_copy(src, dst, store_sem.at[i])
        copy.start()
        return copy

    loads[0].wait()
    payload = place.local_stats(place.own(x_ref))
    place.meet()
    place.ar_start(0, 0, payload)
    place.halo_start(0, xe, True)
    loads[1].wait()
    place.halo_start(1, ue, False)
    for load in loads[2:]:
        load.wait()
    gain1, shift1, gain2, shift2 = (vectors[i] for i in range(4))
    turn(w2_ref, wf2)
    place.stats_stage(0, 0)
    turn(w1_ref, wf1)
    place.halo_wait(0, xe)
    copy_first(place, xe)
    stats1 = place.stats_stage(0, 1)

    build_act(xe, a1, stats1, gain1, shift1)
    for f, value in enumerate(conv(a1, taps_of(w1_ref))):
        he[2 + f, 1 : R + 1] = value.astype(BF16).reshape(R, W, C)
    hidden = place.own_block(he, 2)
    place.ar_start(1, 0, place.local_stats(place.own(hidden)))
    place.halo_wait(1, ue)
    blank_next(place, ue)
    build_grad(ue)
    place.stats_stage(1, 0)
    place.halo_start(2, he, True)
    back_conv(g3, wf2)
    back_first(g3, wf2)
    place.halo_wait(2, he)
    copy_first(place, he)
    stats2 = place.stats_stage(1, 1)

    second = iter(weight_sum(1, wo2_hbm, arrivals[2:], True))
    first = iter(weight_sum(0, wo1_hbm, arrivals[:2], False))
    place.ar_start(2, 0, norm_back_sums(hidden, stats2, gain2, shift2))
    build_act(he, a2, stats2, gain2, shift2)
    place.sums_stage(2, 0)
    weight_grad(a2, u_ref, 1)
    sums2 = place.sums_stage(2, 1)
    for f in range(F):
        value = norm_back_value(hidden, stats2, gain2, sums2, f)
        ge[f, 1 : R + 1] = value.astype(BF16).reshape(R, W, C)
    place.halo_start(3, ge, False)
    next(second)()
    weight_grad(a1, place.own_block(ge, 0), 0)
    next(second)()
    next(first)()
    place.halo_wait(3, ge)
    blank_next(place, ge)
    build_grad(ge)
    next(second)()
    back_conv(g3, wf1)
    back_first(g3, wf1)
    place.ar_start(3, 0, norm_back_sums(x_ref, stats1, gain1, shift1))
    next(first)()
    next(second)()
    branch = conv(a2, taps_of(w2_ref))
    for f in range(F):
        total = x_ref[f].astype(F32).reshape(cells, C) + branch[f]
        out_ref[f] = total.astype(BF16).reshape(R, W, C)
    stores = [store(0, out_ref, out_hbm)]
    next(first)()
    place.sums_stage(3, 0)
    next(second)()
    next(first)()
    next(second)()
    sums1 = place.sums_stage(3, 1)
    for f in range(F):
        value = norm_back_value(x_ref, stats1, gain1, sums1, f)
        total = u_ref[f].astype(F32).reshape(cells, C) + value
        ig_ref[f] = total.astype(BF16).reshape(R, W, C)
    stores.append(store(1, ig_ref, ig_hbm))
    for i, (row, result) in enumerate(zip(sums1 + sums2, (gg1_hbm, sg1_hbm, gg2_hbm, sg2_hbm))):
        results[i] = row
        stores.append(store(2 + i, results.at[i], result))
    next(second)()
    next(first)()
    next(second)()
    next(first)()

    for copy in stores:
        copy.wait()
    next(second)()
    next(first)()
    for k in range(4):
        place.ar_sent(k)
    for q, ref in enumerate((xe, ue, he, ge)):
        place.halo_sent(q, ref)


def finish_kernel(*refs):
    sources, places, (fields, vectors, narrow, wide, load_sem, sem) = refs[:8], refs[8:16], refs[16:]
    copies = []

    def load(i, src, dst):
        copy = pltpu.make_async_copy(src, dst, load_sem.at[i])
        copy.start()
        return copy

    def write(src, dst):
        copy = pltpu.make_async_copy(src, dst, sem.at[len(copies)])
        copy.start()
        copies.append(copy)

    spans = ((0, 9), (9, 10), (19, 9))
    weights = []
    for j, (lo, count) in enumerate(spans):
        for q in range(2):
            rows = pl.ds(lo * C, count * C)
            weights.append(load(2 * j + q, sources[2 + q].at[rows], narrow.at[q, rows]))
    bounce = [(i, fields.at[i]) for i in range(2)] + [(4 + i, vectors.at[i]) for i in range(4)]
    others = [load(6 + n, sources[i], ref) for n, (i, ref) in enumerate(bounce)]
    for j, (lo, count) in enumerate(spans):
        for q in range(2):
            weights[2 * j + q].wait()
            for i in range(3):
                to = (9 * i + 3 * j) * C
                for k in range(3):
                    at = 3 * i + k
                    tap = lo + at + (1 if count == 10 and at >= 5 else 0)
                    block = narrow[q, tap * C : (tap + 1) * C]
                    wide[q, to + k * C : to + (k + 1) * C] = block.astype(F32)
                rows = pl.ds(to, 3 * C)
                write(wide.at[q, rows], places[2 + q].at[rows])
        if j == 0:
            for copy, (i, ref) in zip(others, bounce):
                copy.wait()
                write(ref, places[i])
    for copy in copies:
        copy.wait()


def body(inputs, gain1, shift1, weight1, gain2, shift2, weight2, upstream):
    F, R, W, _ = inputs.shape
    s = plan_of(lax.axis_size("tm"), lax.axis_size("height"), F, R, W)
    E, RE = F + 2, R + 2
    cells = R * W
    hbm = pl.BlockSpec(memory_space=pltpu.HBM)
    field = jax.ShapeDtypeStruct(inputs.shape, BF16)
    weights = jax.ShapeDtypeStruct((s.taps * C, C), BF16)
    vector = jax.ShapeDtypeStruct((1, C), F32)
    wide = pltpu.VMEM((E, RE, W, C), BF16)
    wider = pltpu.VMEM((E, RE, W, 3 * C), BF16)
    arrivals = []
    for first, _, rows, _, _ in s.parts[0]:
        arrivals.append(pltpu.VMEM((s.size[first], rows // s.size[first], C), BF16))
    ((first, _, rows, _, _),) = s.parts[1]
    arrivals.append(pltpu.VMEM((2, rows // s.size[first] // 2, C), BF16))
    arrivals.append(pltpu.VMEM((2, rows // s.size[first], C), BF16))
    room = 60 * 1024 * 1024
    results = pl.pallas_call(
        functools.partial(kernel, s),
        out_shape=[field, field, weights, weights, vector, vector, vector, vector],
        in_specs=[hbm] * 8,
        out_specs=[hbm] * 8,
        scratch_shapes=[
            pltpu.VMEM((27, C, C), BF16),
            pltpu.VMEM((27, C, C), BF16),
            pltpu.VMEM((3, 9 * C, C), BF16),
            pltpu.VMEM((3, 9 * C, C), BF16),
            pltpu.VMEM((4, 1, C), F32),
            pltpu.VMEM((F, R, W, C), BF16),
            pltpu.VMEM((F, R, W, C), BF16),
            pltpu.VMEM((2, s.taps * C, C), BF16),
            pltpu.VMEM((4, 1, C), F32),
            wide,
            wide,
            wide,
            wide,
            wider,
            wider,
            wider,
            pltpu.VMEM((F, cells, C), F32),
            pltpu.VMEM((F, cells, C), F32),
            pltpu.VMEM((8, max(s.stages), 2, C), F32),
            pltpu.VMEM((2, s.taps * C, C), BF16),
            pltpu.VMEM((2, s.half, C), BF16),
            pltpu.VMEM((2, s.half, C), BF16),
            pltpu.VMEM((2, 4 * s.nz, s.tile, C), BF16),
            arrivals,
            pltpu.SemaphoreType.DMA((8,)),
            pltpu.SemaphoreType.DMA((8,)),
            pltpu.SemaphoreType.DMA((4,)),
            pltpu.SemaphoreType.DMA((4,)),
            pltpu.SemaphoreType.DMA((2, 17)),
            pltpu.SemaphoreType.DMA((2, 17)),
            pltpu.SemaphoreType.DMA((8,)),
            pltpu.SemaphoreType.DMA((8,)),
        ],
        compiler_params=pltpu.CompilerParams(
            collective_id=0, has_side_effects=True, vmem_limit_bytes=room
        ),
        cost_estimate=pl.CostEstimate(
            flops=6 * 2 * F * cells * 27 * C * C, bytes_accessed=8_000_000, transcendentals=1_000_000
        ),
    )(
        inputs,
        upstream,
        weight1.reshape(27, C, C),
        weight2.reshape(27, C, C),
        gain1.reshape(1, C),
        shift1.reshape(1, C),
        gain2.reshape(1, C),
        shift2.reshape(1, C),
    )
    total = jax.ShapeDtypeStruct((27 * C, C), F32)
    output, input_grad, first, second, gg1, sg1, gg2, sg2 = pl.pallas_call(
        finish_kernel,
        out_shape=[field, field, total, total, vector, vector, vector, vector],
        in_specs=[hbm] * 8,
        out_specs=[hbm] * 8,
        scratch_shapes=[
            pltpu.VMEM((2, F, R, W, C), BF16),
            pltpu.VMEM((4, 1, C), F32),
            pltpu.VMEM((2, s.taps * C, C), BF16),
            pltpu.VMEM((2, 27 * C, C), F32),
            pltpu.SemaphoreType.DMA((12,)),
            pltpu.SemaphoreType.DMA((24,)),
        ],
        compiler_params=pltpu.CompilerParams(vmem_limit_bytes=room),
        cost_estimate=pl.CostEstimate(flops=0, bytes_accessed=6_000_000, transcendentals=0),
    )(*results)
    return (
        output,
        input_grad,
        first.reshape(3, 3, 3, C, C),
        second.reshape(3, 3, 3, C, C),
        gg1.reshape(C),
        sg1.reshape(C),
        gg2.reshape(C),
        sg2.reshape(C),
    )


def solution(mesh):
    fields = P("tm", "height", None, None)
    return jax.shard_map(
        body,
        mesh=mesh,
        in_specs=(fields, P(), P(), P(), P(), P(), P(), fields),
        out_specs=(fields, fields, P(), P(), P(), P(), P(), P()),
        check_vma=False,
    )
```

```python
import functools
import types

import jax
import jax.numpy as jnp
from jax import lax
from jax.experimental import pallas as pl
from jax.experimental.pallas import tpu as pltpu
from jax.sharding import PartitionSpec as P

C = 128
G = 32
MEMBERS = C // G
EPSILON = 1e-06
MESH = pl.DeviceIdType.MESH
F32 = jnp.float32
BF16 = jnp.bfloat16


def plan_of(tm, height, frames, rows, columns):
    s = types.SimpleNamespace()
    s.tm, s.nz = tm, height
    s.nyx = tm // 2
    s.nx = 4 if s.nyx >= 16 else 2
    s.ny = s.nyx // s.nx
    s.frames, s.rows, s.columns = frames, rows, columns
    s.stages = (2 * s.nz, s.nyx)
    s.taps = 28
    s.half = s.taps * C // 2
    most = min(s.nz - 1, 7) if s.nz > 2 else 2
    s.parts = (
        (("x", "y", 1024, 0, s.nz // 2), ("y", "x", s.half - 1024, s.nz // 2, most - s.nz // 2)),
        (("y", "x", s.half, 0, most),),
    )
    s.size = {"y": s.ny, "x": s.nx}
    s.tile = max(
        rows // s.size[first] // (s.size[second] * count)
        for parts in s.parts
        for first, second, rows, _, count in parts
    )
    return s


def bundle(sem, ref):
    pltpu.make_async_copy(ref, ref, sem).wait()


def group_total(row):
    lane = lax.broadcasted_iota(jnp.int32, row.shape, 1)
    for step in (1, 2):
        ahead = pltpu.roll(row, C - step, 1)
        behind = pltpu.roll(row, step, 1)
        row = row + jnp.where(lane & step == 0, ahead, behind)
    return row


def wrap(i, n):
    return jnp.where(i >= n, i - n, i)


def sigmoid(u):
    return 1.0 / (1.0 + jnp.exp(-u))


class Place:
    def __init__(self, s):
        self.s = s
        self.tm = tm = lax.axis_index("tm")
        self.z = z = lax.axis_index("height")
        self.core = core = tm % 2
        self.yx = yx = tm // 2
        self.x = yx % s.nx
        self.y = yx // s.nx
        self.mate_tm = mate_tm = tm + 1 - 2 * core
        self.z_ring = z_ring = [z] + [wrap(z + d, s.nz) for d in range(1, s.nz)]
        self.x_ring = [self.x] + [wrap(self.x + d, s.nx) for d in range(1, s.nx)]
        self.y_ring = [self.y] + [wrap(self.y + d, s.ny) for d in range(1, s.ny)]
        self.rings = {"y": self.y_ring, "x": self.x_ring}
        self.row = [self.tm_of(self.y, q, core) for q in self.x_ring]
        self.column = [self.tm_of(q, self.x, core) for q in self.y_ring]
        self.lines = {"y": self.column, "x": self.row}
        self.groups = (
            (core * s.nz + z, [(tm, q) for q in z_ring[1:]] + [(mate_tm, q) for q in z_ring]),
            (yx, [(wrap(yx + d, s.nyx) * 2 + core, z) for d in range(1, s.nyx)]),
        )
        self.tm_next, self.tm_prev = wrap(tm + 1, s.tm), wrap(tm + s.tm - 1, s.tm)
        self.z_next, self.z_prev = z_ring[1], z_ring[-1]
        self.partners = [peer for _, peers in self.groups for peer in peers]
        self.partners = self.partners + [
            (t, q) for t in (self.tm_next, self.tm_prev) for q in (z, self.z_next, self.z_prev)
        ]
        self.partners = self.partners + [
            (t, q) for line in (self.row, self.column) for t in line[1:] for q in z_ring[1:]
        ]

    def tm_of(self, y, x, core):
        return (y * self.s.nx + x) * 2 + core

    def greet(self):
        barrier = pltpu.get_barrier_semaphore()
        for partner in self.partners:
            pl.semaphore_signal(barrier, inc=1, device_id=partner, device_id_type=MESH)

    def meet(self):
        pl.semaphore_wait(pltpu.get_barrier_semaphore(), len(self.partners))

    def own_block(self, ref, lo):
        return ref.at[pl.ds(lo, self.s.frames), pl.ds(1, self.s.rows)]

    def own(self, ref):
        return ref[...].astype(F32).reshape(-1, C)

    def bind(self, ar, ar_send, ar_recv, halo_send, halo_recv):
        self.ar, self.ar_send, self.ar_recv = ar, ar_send, ar_recv
        self.halo_send, self.halo_recv = halo_send, halo_recv

    def ar_start(self, k, stage, payload):
        i = 2 * k + stage
        slot, peers = self.groups[stage]
        self.ar[i, slot, 0:1] = payload[0]
        self.ar[i, slot, 1:2] = payload[1]
        for peer in peers:
            pltpu.make_async_remote_copy(
                src_ref=self.ar.at[i, slot],
                dst_ref=self.ar.at[i, slot],
                send_sem=self.ar_send.at[i],
                recv_sem=self.ar_recv.at[i],
                device_id=peer,
                device_id_type=MESH,
            ).start()

    def ar_wait(self, k, stage):
        i = 2 * k + stage
        n = self.s.stages[stage]
        bundle(self.ar_recv.at[i], self.ar.at[i, pl.ds(0, n - 1)])
        parts = [self.ar[i, j] for j in range(n)]
        return [p[0:1] for p in parts], [p[1:2] for p in parts]

    def ar_sent(self, k):
        for stage, n in enumerate(self.s.stages):
            i = 2 * k + stage
            bundle(self.ar_send.at[i], self.ar.at[i, pl.ds(0, n - 1)])

    def local_count(self):
        return float(self.s.frames * self.s.rows * self.s.columns * MEMBERS)

    def local_stats(self, v):
        centre = group_total(jnp.sum(v, axis=0, keepdims=True)) / self.local_count()
        spread = group_total(jnp.sum((v - centre) ** 2, axis=0, keepdims=True))
        return centre, spread

    def join_stats(self, parts, count):
        means, spreads = parts
        centre = sum(means) / float(len(means))
        spread = sum(spreads) + count * sum((mean - centre) ** 2 for mean in means)
        return centre, spread

    def stats_stage(self, k, stage):
        count = self.local_count()
        for n in self.s.stages[:stage]:
            count = count * n
        joined = self.join_stats(self.ar_wait(k, stage), count)
        if stage < 1:
            return self.ar_start(k, stage + 1, joined)
        centre, spread = joined
        return centre, lax.rsqrt(spread / (count * self.s.stages[stage]) + EPSILON)

    def sums_stage(self, k, stage):
        first, second = self.ar_wait(k, stage)
        totals = sum(first), sum(second)
        return totals if stage == 1 else self.ar_start(k, stage + 1, totals)

    def halo_start(self, q, ref, ahead):
        F, R, z = self.s.frames, self.s.rows, self.z
        target = self.tm_next if ahead else self.tm_prev
        far, near = (0, 2) if ahead else (2, 0)
        frames = pl.ds(near, F)
        everything = ref.at[frames, pl.ds(1, R)]
        top, bottom = ref.at[frames, pl.ds(1, 1)], ref.at[frames, pl.ds(R, 1)]
        copies = [
            (everything, ref.at[pl.ds(far, F), pl.ds(1, R)], (target, z)),
            (top, ref.at[pl.ds(near, F), pl.ds(R + 1, 1)], (self.tm, self.z_prev)),
            (bottom, ref.at[pl.ds(near, F), pl.ds(0, 1)], (self.tm, self.z_next)),
            (top, ref.at[pl.ds(far, F), pl.ds(R + 1, 1)], (target, self.z_prev)),
            (bottom, ref.at[pl.ds(far, F), pl.ds(0, 1)], (target, self.z_next)),
        ]
        for piece, place, device in copies:
            pltpu.make_async_remote_copy(
                src_ref=piece,
                dst_ref=place,
                send_sem=self.halo_send.at[q],
                recv_sem=self.halo_recv.at[q],
                device_id=device,
                device_id_type=MESH,
            ).start()

    def halo_bytes(self, sem, ref):
        F, R = self.s.frames, self.s.rows
        bundle(sem, ref.at[pl.ds(0, F + 2), pl.ds(0, F * (R + 4) // (F + 2))])

    def halo_wait(self, q, ref):
        self.halo_bytes(self.halo_recv.at[q], ref)

    def halo_sent(self, q, ref):
        self.halo_bytes(self.halo_send.at[q], ref)


def blank_next(place, ref):
    F = place.s.frames

    @pl.when(place.tm == place.s.tm - 1)
    def _():
        ref[F : F + 2] = jnp.zeros((2,) + ref.shape[1:], ref.dtype)


def copy_first(place, ref):
    @pl.when(place.tm == 0)
    def _():
        ref[0] = ref[2]
        ref[1] = ref[2]


def kernel(
    s,
    x_hbm,
    u_hbm,
    w1_hbm,
    w2_hbm,
    g1_hbm,
    s1_hbm,
    g2_hbm,
    s2_hbm,
    out_hbm,
    ig_hbm,
    wo1_hbm,
    wo2_hbm,
    gg1_hbm,
    sg1_hbm,
    gg2_hbm,
    sg2_hbm,
    w1_ref,
    w2_ref,
    wf1,
    wf2,
    vectors,
    out_ref,
    ig_ref,
    wo,
    results,
    xe,
    ue,
    he,
    ge,
    a1,
    a2,
    g3,
    dact,
    pre_buf,
    ar,
    wg,
    r1,
    p1,
    rx,
    arrivals,
    ar_send,
    ar_recv,
    halo_send,
    halo_recv,
    w_send,
    w_recv,
    load_sem,
    store_sem,
):
    F, R, W = s.frames, s.rows, s.columns
    E, RE = F + 2, R + 2
    cells = R * W
    place = Place(s)
    place.bind(ar, ar_send, ar_recv, halo_send, halo_recv)
    tm, z, x, y, core = place.tm, place.z, place.x, place.y, place.core
    mate_tm, z_ring = place.mate_tm, place.z_ring

    x_ref, u_ref = place.own_block(xe, 2), place.own_block(ue, 0)
    loads = [
        (x_hbm, x_ref),
        (u_hbm, u_ref),
        (w1_hbm, w1_ref),
        (w2_hbm, w2_ref),
        (g1_hbm, vectors.at[0]),
        (s1_hbm, vectors.at[1]),
        (g2_hbm, vectors.at[2]),
        (s2_hbm, vectors.at[3]),
    ]
    loads = [pltpu.make_async_copy(a, b, load_sem.at[i]) for i, (a, b) in enumerate(loads)]
    for load in loads:
        load.start()
    place.greet()

    def shifted(v, dst, f):
        column = lax.broadcasted_iota(jnp.int32, v.shape, 0) & (W - 1)
        left = jnp.where(column == 0, 0.0, pltpu.roll(v, 1, 0))
        right = jnp.where(column == W - 1, 0.0, pltpu.roll(v, RE * W - 1, 0))
        for k, piece in enumerate((left, v, right)):
            dst[f, :, :, k * C : (k + 1) * C] = piece.astype(BF16).reshape(RE, W, C)

    def blank_rows(dst):
        blank = jnp.zeros((E, 1) + dst.shape[2:], dst.dtype)

        @pl.when(z == 0)
        def _():
            dst[:, 0:1] = blank

        @pl.when(z == s.nz - 1)
        def _():
            dst[:, R + 1 : R + 2] = blank

    def build_act(src, dst, stats, gain, shift):
        centre, inverse = stats
        scale = inverse * gain

        def frame(f, carry):
            v = src[f].astype(F32).reshape(RE * W, C)
            affine = (v - centre) * scale + shift
            shifted(affine * sigmoid(affine), dst, f)
            return carry

        lax.fori_loop(0, E, frame, 0)
        blank_rows(dst)

    def build_grad(src):
        def frame(f, carry):
            shifted(src[f].astype(F32).reshape(RE * W, C), g3, f)
            return carry

        lax.fori_loop(0, E, frame, 0)
        blank_rows(g3)

    def dot(a, b):
        return jnp.dot(a, b, preferred_element_type=F32)

    def turn(src, dst):
        for at in range(27):
            dst[at // 9, (at % 9) * C : (at % 9 + 1) * C, :] = src[26 - at].T

    def patches(src, f):
        return jnp.concatenate([src[f, j : j + R].reshape(cells, 3 * C) for j in range(3)], axis=1)

    def conv(src, taps):
        first = dot(patches(src, 0), taps[0])
        second = None
        for f in (1, 2):
            both = dot(patches(src, f), jnp.concatenate([taps[f], taps[f - 1]], axis=1))
            first = first + both[:, :C]
            second = both[:, C:] if second is None else second + both[:, C:]
        return first, second + dot(patches(src, 3), taps[2])

    def taps_of(weight):
        return [weight[9 * i : 9 * i + 9].reshape(9 * C, C) for i in range(3)]

    def back_conv(src, weight):
        dact[0], dact[1] = conv(src, [weight[i] for i in range(3)])

    def back_first(src, weight):
        @pl.when(tm == 0)
        def _():
            both = dot(patches(src, 0), jnp.concatenate([weight[1], weight[2]], axis=1))
            dact[0] += both[:, :C] + both[:, C:] + dot(patches(src, 1), weight[2])

    def weight_grad(act, grad, q):
        turned = [grad[f].reshape(cells, C).T for f in range(F)]
        both = jnp.concatenate(turned, axis=0)
        wg[q, 14 * C : 15 * C, :] = jnp.zeros((C, C), BF16)
        mate = (mate_tm, z)

        def row_tap(j, base):
            window = [act[f, pl.ds(j, R)].reshape(cells, 3 * C) for f in range(E)]
            one, two = dot(both, window[1]), dot(both, window[2])
            sums = (
                dot(turned[0], window[0]) + one[C:],
                one[:C] + two[C:],
                two[:C] + dot(turned[1], window[3]),
            )
            for i, total in enumerate(sums):
                total = total.astype(BF16)
                for k in range(3):
                    at = 3 * i + k
                    lo = base(at) * C
                    wg[q, pl.ds(pl.multiple_of(lo, C), C), :] = total[:, k * C : (k + 1) * C]

        def send(i, src, dst, taps):
            pltpu.make_async_remote_copy(
                src_ref=wg.at[q, pl.ds(pl.multiple_of(src * C, C), taps * C)],
                dst_ref=r1.at[q, pl.ds(pl.multiple_of(dst * C, C), taps * C)],
                send_sem=w_send.at[q, i],
                recv_sem=w_recv.at[q, i],
                device_id=mate,
                device_id_type=MESH,
            ).start()

        row_tap(2 - 2 * core, lambda at: (1 - core) * 19 + at)
        send(0, (1 - core) * 19, (1 - core) * 5, 9)
        row_tap(1, lambda at: 9 + at if at < 5 else 10 + at)
        send(1, 14 - core * 5, core * 9, 5)
        row_tap(2 * core, lambda at: core * 19 + at)

    def norm_back_sums(values, stats, gain, shift):
        centre, inverse = stats
        total_cross = jnp.zeros((1, C), F32)
        total = jnp.zeros((1, C), F32)
        for f in range(F):
            normed = (values[f].astype(F32).reshape(cells, C) - centre) * inverse
            affine = normed * gain + shift
            sig = sigmoid(affine)
            pre = dact[f] * sig * (1.0 + affine * (1.0 - sig))
            pre_buf[f] = pre
            total_cross += jnp.sum(pre * normed, axis=0, keepdims=True)
            total += jnp.sum(pre, axis=0, keepdims=True)
        return total_cross, total

    def norm_back_value(values, stats, gain, sums, f):
        centre, inverse = stats
        gain_grad, shift_grad = sums
        members = float(F * cells * MEMBERS * s.tm * s.nz)
        mean_grad = group_total(gain * shift_grad) / members
        mean_cross = group_total(gain * gain_grad) / members
        normed = (values[f].astype(F32).reshape(cells, C) - centre) * inverse
        return inverse * (pre_buf[f] * gain - mean_grad - normed * mean_cross)

    def weight_sum(q, home, arrivals, relay):
        out = wo.at[q]
        mate = (mate_tm, z)
        mine = core * s.half
        spot = {"y": y, "x": x}
        parts = []
        lo = at = 0
        for p, (first, second, rows, z_lo, z_count) in enumerate(s.parts[q]):
            part = types.SimpleNamespace(p=p, first=first, second=second, lo=lo, at=at, z_lo=z_lo)
            part.zs = range(z_lo, z_lo + z_count)
            part.n = s.size[first]
            part.one = rows // part.n
            part.tile = part.one // (s.size[second] * z_count)
            part.ring, part.line = place.rings[first], place.lines[first]
            part.owner = jnp.logical_and(z >= z_lo, z < z_lo + z_count)
            part.slot = z * s.size[second] + spot[second]
            part.own = ((z - z_lo) * s.size[second] + spot[second]) * part.tile
            lo, at = lo + rows, at + part.one
            parts.append(part)
        plane = s.nz * 4

        def span(lo, rows):
            return pl.ds(pl.multiple_of(lo, 16), rows)

        def send(i, src, dst, device, arrival=None):
            pltpu.make_async_remote_copy(
                src_ref=src,
                dst_ref=dst,
                send_sem=w_send.at[q, i],
                recv_sem=w_recv.at[q, i if arrival is None else arrival],
                device_id=device,
                device_id_type=MESH,
            ).start()

        def arrived(i, rows):
            bundle(w_recv.at[q, i], wg.at[q, pl.ds(0, rows)])

        def sent(i, rows):
            bundle(w_send.at[q, i], wg.at[q, pl.ds(0, rows)])

        def add_mate(part):
            def piece(t, carry):
                rows = span(t * C, C)
                kept = wg[q, span(mine + t * C, C)].astype(F32)
                p1[q, rows] = (kept + r1[q, rows].astype(F32)).astype(BF16)
                return carry

            lax.fori_loop(part.lo // C, (part.lo + part.n * part.one) // C, piece, 0)

        def rows_of(part, i, skip=0, rows=None):
            return span(part.lo + i * part.one + skip, part.one if rows is None else rows)

        def step_mate():
            arrived(0, 9 * C)
            arrived(1, 5 * C)
            for part in parts:
                add_mate(part)
                if relay:
                    half = part.one // 2
                    far = part.ring[2]
                    one = p1.at[q, rows_of(part, far, 0, half)]
                    two = p1.at[q, rows_of(part, far, half, half)]
                    send(2, one, arrivals[0].at[0], (part.line[1], z))
                    send(2, two, arrivals[0].at[1], (part.line[3], z))
                else:
                    for d in range(1, part.n):
                        src = p1.at[q, rows_of(part, part.ring[d])]
                        dst = arrivals[part.p].at[part.ring[0]]
                        send(2 + part.p, src, dst, (part.line[d], z))

        def step_relay():
            (part,) = parts
            half = part.one // 2
            arrived(2, part.one)
            for side, to, skip in ((0, 1, 0), (1, 3, half)):
                rows = rows_of(part, part.ring[to], skip, half)
                total = p1[q, rows].astype(F32) + arrivals[0][side].astype(F32)
                p1[q, rows] = total.astype(BF16)
            for side, to in ((0, 1), (1, 3)):
                src = p1.at[q, rows_of(part, part.ring[to])]
                send(3, src, arrivals[1].at[side], (part.line[to], z))

        def step_plane():
            for part in parts:
                total = p1[q, rows_of(part, part.ring[0])].astype(F32)
                if relay:
                    arrived(3, 2 * part.one)
                    total += arrivals[1][0].astype(F32) + arrivals[1][1].astype(F32)
                else:
                    arrived(2 + part.p, (part.n - 1) * part.one)
                    for d in range(1, part.n):
                        total += arrivals[part.p][part.ring[d]].astype(F32)
                r1[q, part.at : part.at + part.one] = total.astype(BF16)
                across, line = place.rings[part.second], place.lines[part.second]
                for d in range(s.size[part.second]):
                    for owner_z in part.zs:

                        def go(part=part, d=d, owner_z=owner_z, across=across, line=line):
                            tile = (owner_z - part.z_lo) * s.size[part.second] + across[d]
                            src = r1.at[q, span(part.at + tile * part.tile, part.tile)]
                            dst = rx.at[q, part.slot, pl.ds(0, part.tile)]
                            send(4 + part.p, src, dst, (line[d], owner_z), 4)

                        if d:
                            go()
                        else:
                            pl.when(z != owner_z)(go)

        def step_own():
            for part in parts:

                @pl.when(part.owner)
                def _(part=part):
                    arrived(4, (plane - 1) * part.tile)
                    tile = pl.ds(0, part.tile)
                    rx[q, part.slot, tile] = r1[q, span(part.at + part.own, part.tile)]
                    total = rx[q, 0, tile].astype(F32)
                    for j in range(1, plane):
                        total += rx[q, j, tile].astype(F32)
                    lo = mine + part.lo + part.ring[0] * part.one + part.own
                    rows = span(lo, part.tile)
                    out[rows] = total.astype(BF16)
                    for t, column in enumerate(place.lines[part.second]):
                        for d, other in enumerate(z_ring):
                            if t or d:
                                send(6 + part.p, out.at[rows], out.at[rows], (column, other))

        def chunk(part, i, skip=0, rows=None):
            return span(mine + part.lo + i * part.one + skip, part.one if rows is None else rows)

        def step_ring():
            for part in parts:

                @pl.when(part.owner)
                def _(part=part):
                    arrived(6 + part.p, part.one - part.tile)

                @pl.when(jnp.logical_not(part.owner))
                def _(part=part):
                    arrived(6 + part.p, part.one)

                rows = chunk(part, part.ring[0])
                for d in (1, 3) if relay else range(1, part.n):
                    send(8 + part.p, out.at[rows], out.at[rows], (part.line[d], z))

        def step_relay_back():
            (part,) = parts
            half = part.one // 2
            arrived(8, 2 * part.one)
            rows = chunk(part, part.ring[3], 0, half)
            send(9, out.at[rows], out.at[rows], (part.line[1], z))
            rows = chunk(part, part.ring[1], half, half)
            send(9, out.at[rows], out.at[rows], (part.line[3], z))

        def keep():
            return pltpu.make_async_copy(
                out.at[span(mine, s.half)], home.at[span(mine, s.half)], store_sem.at[6 + q]
            )

        def step_deliver():
            for part in parts:
                if relay:
                    arrived(9, part.one)
                else:
                    arrived(8 + part.p, (part.n - 1) * part.one)
                rows = span(mine + part.lo, part.n * part.one)
                send(16, out.at[rows], home.at[rows], mate)
            keep().start()

        def step_end():
            arrived(16, s.half)
            keep().wait()

        def finish():
            sent(0, 9 * C)
            sent(1, 5 * C)
            sent(16, s.half)
            for part in parts:
                if relay:
                    sent(2, part.one)
                    sent(3, 2 * part.one)
                    sent(8, 2 * part.one)
                    sent(9, part.one)
                else:
                    sent(2 + part.p, (part.n - 1) * part.one)
                    sent(8 + part.p, (part.n - 1) * part.one)

                @pl.when(part.owner)
                def _(part=part):
                    sent(4 + part.p, part.one - part.tile)
                    sent(6 + part.p, (plane - 1) * part.tile)

                @pl.when(jnp.logical_not(part.owner))
                def _(part=part):
                    sent(4 + part.p, part.one)

        if relay:
            steps = [step_mate, step_relay, step_plane, step_own, step_ring, step_relay_back]
        else:
            steps = [step_mate, step_plane, step_own, step_ring]
        return steps + [step_deliver, step_end, finish]

    def store(i, src, dst):
        copy = pltpu.make_async_copy(src, dst, store_sem.at[i])
        copy.start()
        return copy

    loads[0].wait()
    payload = place.local_stats(place.own(x_ref))
    place.meet()
    place.ar_start(0, 0, payload)
    place.halo_start(0, xe, True)
    loads[1].wait()
    place.halo_start(1, ue, False)
    for load in loads[2:]:
        load.wait()
    gain1, shift1, gain2, shift2 = (vectors[i] for i in range(4))
    turn(w2_ref, wf2)
    place.stats_stage(0, 0)
    turn(w1_ref, wf1)
    place.halo_wait(0, xe)
    copy_first(place, xe)
    stats1 = place.stats_stage(0, 1)

    build_act(xe, a1, stats1, gain1, shift1)
    for f, value in enumerate(conv(a1, taps_of(w1_ref))):
        he[2 + f, 1 : R + 1] = value.astype(BF16).reshape(R, W, C)
    hidden = place.own_block(he, 2)
    place.ar_start(1, 0, place.local_stats(place.own(hidden)))
    place.halo_wait(1, ue)
    blank_next(place, ue)
    build_grad(ue)
    place.stats_stage(1, 0)
    place.halo_start(2, he, True)
    back_conv(g3, wf2)
    back_first(g3, wf2)
    place.halo_wait(2, he)
    copy_first(place, he)
    stats2 = place.stats_stage(1, 1)

    second = iter(weight_sum(1, wo2_hbm, arrivals[2:], True))
    first = iter(weight_sum(0, wo1_hbm, arrivals[:2], False))
    place.ar_start(2, 0, norm_back_sums(hidden, stats2, gain2, shift2))
    build_act(he, a2, stats2, gain2, shift2)
    place.sums_stage(2, 0)
    weight_grad(a2, u_ref, 1)
    sums2 = place.sums_stage(2, 1)
    for f in range(F):
        value = norm_back_value(hidden, stats2, gain2, sums2, f)
        ge[f, 1 : R + 1] = value.astype(BF16).reshape(R, W, C)
    place.halo_start(3, ge, False)
    next(second)()
    weight_grad(a1, place.own_block(ge, 0), 0)
    next(second)()
    next(first)()
    place.halo_wait(3, ge)
    blank_next(place, ge)
    build_grad(ge)
    back_conv(g3, wf1)
    back_first(g3, wf1)
    place.ar_start(3, 0, norm_back_sums(x_ref, stats1, gain1, shift1))
    next(second)()
    next(first)()
    branch = conv(a2, taps_of(w2_ref))
    for f in range(F):
        total = x_ref[f].astype(F32).reshape(cells, C) + branch[f]
        out_ref[f] = total.astype(BF16).reshape(R, W, C)
    stores = [store(0, out_ref, out_hbm)]
    place.sums_stage(3, 0)
    next(second)()
    next(first)()
    sums1 = place.sums_stage(3, 1)
    for f in range(F):
        value = norm_back_value(x_ref, stats1, gain1, sums1, f)
        total = u_ref[f].astype(F32).reshape(cells, C) + value
        ig_ref[f] = total.astype(BF16).reshape(R, W, C)
    stores.append(store(1, ig_ref, ig_hbm))
    for i, (row, result) in enumerate(zip(sums1 + sums2, (gg1_hbm, sg1_hbm, gg2_hbm, sg2_hbm))):
        results[i] = row
        stores.append(store(2 + i, results.at[i], result))
    next(second)()
    next(first)()
    next(second)()
    next(first)()
    next(second)()
    next(first)()
    next(second)()

    for copy in stores:
        copy.wait()
    next(second)()
    next(first)()
    for k in range(4):
        place.ar_sent(k)
    for q, ref in enumerate((xe, ue, he, ge)):
        place.halo_sent(q, ref)


def finish_kernel(*refs):
    sources, places, (fields, vectors, narrow, wide, load_sem, sem) = refs[:8], refs[8:16], refs[16:]
    copies = []

    def load(i, src, dst):
        copy = pltpu.make_async_copy(src, dst, load_sem.at[i])
        copy.start()
        return copy

    def write(src, dst):
        copy = pltpu.make_async_copy(src, dst, sem.at[len(copies)])
        copy.start()
        copies.append(copy)

    spans = ((0, 9), (9, 10), (19, 9))
    weights = []
    for j, (lo, count) in enumerate(spans):
        for q in range(2):
            rows = pl.ds(lo * C, count * C)
            weights.append(load(2 * j + q, sources[2 + q].at[rows], narrow.at[q, rows]))
    bounce = [(i, fields.at[i]) for i in range(2)] + [(4 + i, vectors.at[i]) for i in range(4)]
    others = [load(6 + n, sources[i], ref) for n, (i, ref) in enumerate(bounce)]
    for j, (lo, count) in enumerate(spans):
        for q in range(2):
            weights[2 * j + q].wait()
            for i in range(3):
                to = (9 * i + 3 * j) * C
                for k in range(3):
                    at = 3 * i + k
                    tap = lo + at + (1 if count == 10 and at >= 5 else 0)
                    block = narrow[q, tap * C : (tap + 1) * C]
                    wide[q, to + k * C : to + (k + 1) * C] = block.T.astype(F32)
                rows = pl.ds(to, 3 * C)
                write(wide.at[q, rows], places[2 + q].at[rows])
        if j == 0:
            for copy, (i, ref) in zip(others, bounce):
                copy.wait()
                write(ref, places[i])
    for copy in copies:
        copy.wait()


def body(inputs, gain1, shift1, weight1, gain2, shift2, weight2, upstream):
    F, R, W, _ = inputs.shape
    s = plan_of(lax.axis_size("tm"), lax.axis_size("height"), F, R, W)
    E, RE = F + 2, R + 2
    cells = R * W
    hbm = pl.BlockSpec(memory_space=pltpu.HBM)
    field = jax.ShapeDtypeStruct(inputs.shape, BF16)
    weights = jax.ShapeDtypeStruct((s.taps * C, C), BF16)
    vector = jax.ShapeDtypeStruct((1, C), F32)
    wide = pltpu.VMEM((E, RE, W, C), BF16)
    wider = pltpu.VMEM((E, RE, W, 3 * C), BF16)
    arrivals = []
    for first, _, rows, _, _ in s.parts[0]:
        arrivals.append(pltpu.VMEM((s.size[first], rows // s.size[first], C), BF16))
    ((first, _, rows, _, _),) = s.parts[1]
    arrivals.append(pltpu.VMEM((2, rows // s.size[first] // 2, C), BF16))
    arrivals.append(pltpu.VMEM((2, rows // s.size[first], C), BF16))
    room = 60 * 1024 * 1024
    results = pl.pallas_call(
        functools.partial(kernel, s),
        out_shape=[field, field, weights, weights, vector, vector, vector, vector],
        in_specs=[hbm] * 8,
        out_specs=[hbm] * 8,
        scratch_shapes=[
            pltpu.VMEM((27, C, C), BF16),
            pltpu.VMEM((27, C, C), BF16),
            pltpu.VMEM((3, 9 * C, C), BF16),
            pltpu.VMEM((3, 9 * C, C), BF16),
            pltpu.VMEM((4, 1, C), F32),
            pltpu.VMEM((F, R, W, C), BF16),
            pltpu.VMEM((F, R, W, C), BF16),
            pltpu.VMEM((2, s.taps * C, C), BF16),
            pltpu.VMEM((4, 1, C), F32),
            wide,
            wide,
            wide,
            wide,
            wider,
            wider,
            wider,
            pltpu.VMEM((F, cells, C), F32),
            pltpu.VMEM((F, cells, C), F32),
            pltpu.VMEM((8, max(s.stages), 2, C), F32),
            pltpu.VMEM((2, s.taps * C, C), BF16),
            pltpu.VMEM((2, s.half, C), BF16),
            pltpu.VMEM((2, s.half, C), BF16),
            pltpu.VMEM((2, 4 * s.nz, s.tile, C), BF16),
            arrivals,
            pltpu.SemaphoreType.DMA((8,)),
            pltpu.SemaphoreType.DMA((8,)),
            pltpu.SemaphoreType.DMA((4,)),
            pltpu.SemaphoreType.DMA((4,)),
            pltpu.SemaphoreType.DMA((2, 17)),
            pltpu.SemaphoreType.DMA((2, 17)),
            pltpu.SemaphoreType.DMA((8,)),
            pltpu.SemaphoreType.DMA((8,)),
        ],
        compiler_params=pltpu.CompilerParams(
            collective_id=0, has_side_effects=True, vmem_limit_bytes=room
        ),
        cost_estimate=pl.CostEstimate(
            flops=6 * 2 * F * cells * 27 * C * C, bytes_accessed=8_000_000, transcendentals=1_000_000
        ),
    )(
        inputs,
        upstream,
        weight1.reshape(27, C, C),
        weight2.reshape(27, C, C),
        gain1.reshape(1, C),
        shift1.reshape(1, C),
        gain2.reshape(1, C),
        shift2.reshape(1, C),
    )
    total = jax.ShapeDtypeStruct((27 * C, C), F32)
    output, input_grad, first, second, gg1, sg1, gg2, sg2 = pl.pallas_call(
        finish_kernel,
        out_shape=[field, field, total, total, vector, vector, vector, vector],
        in_specs=[hbm] * 8,
        out_specs=[hbm] * 8,
        scratch_shapes=[
            pltpu.VMEM((2, F, R, W, C), BF16),
            pltpu.VMEM((4, 1, C), F32),
            pltpu.VMEM((2, s.taps * C, C), BF16),
            pltpu.VMEM((2, 27 * C, C), F32),
            pltpu.SemaphoreType.DMA((12,)),
            pltpu.SemaphoreType.DMA((24,)),
        ],
        compiler_params=pltpu.CompilerParams(vmem_limit_bytes=room),
        cost_estimate=pl.CostEstimate(flops=0, bytes_accessed=6_000_000, transcendentals=0),
    )(*results)
    return (
        output,
        input_grad,
        first.reshape(3, 3, 3, C, C),
        second.reshape(3, 3, 3, C, C),
        gg1.reshape(C),
        sg1.reshape(C),
        gg2.reshape(C),
        sg2.reshape(C),
    )


def solution(mesh):
    fields = P("tm", "height", None, None)
    return jax.shard_map(
        body,
        mesh=mesh,
        in_specs=(fields, P(), P(), P(), P(), P(), P(), fields),
        out_specs=(fields, fields, P(), P(), P(), P(), P(), P()),
        check_vma=False,
    )
```

```python
import functools
import types

import jax
import jax.numpy as jnp
from jax import lax
from jax.experimental import pallas as pl
from jax.experimental.pallas import tpu as pltpu
from jax.sharding import PartitionSpec as P

C = 128
G = 32
MEMBERS = C // G
EPSILON = 1e-06
MESH = pl.DeviceIdType.MESH
F32 = jnp.float32
BF16 = jnp.bfloat16


def plan_of(tm, height, frames, rows, columns):
    s = types.SimpleNamespace()
    s.tm, s.nz = tm, height
    s.nyx = tm // 2
    s.nx = 4 if s.nyx >= 16 else 2
    s.ny = s.nyx // s.nx
    s.frames, s.rows, s.columns = frames, rows, columns
    s.stages = (2 * s.nz, s.nyx)
    s.taps = 28
    s.half = s.taps * C // 2
    most = min(s.nz - 1, 7) if s.nz > 2 else 2
    s.parts = (
        (("x", "y", 1024, 0, s.nz // 2), ("y", "x", s.half - 1024, s.nz // 2, most - s.nz // 2)),
        (("y", "x", s.half, 0, most),),
    )
    s.size = {"y": s.ny, "x": s.nx}
    s.tile = max(
        rows // s.size[first] // (s.size[second] * count)
        for parts in s.parts
        for first, second, rows, _, count in parts
    )
    return s


def bundle(sem, ref):
    pltpu.make_async_copy(ref, ref, sem).wait()


def group_total(row):
    lane = lax.broadcasted_iota(jnp.int32, row.shape, 1)
    for step in (1, 2):
        ahead = pltpu.roll(row, C - step, 1)
        behind = pltpu.roll(row, step, 1)
        row = row + jnp.where(lane & step == 0, ahead, behind)
    return row


def wrap(i, n):
    return jnp.where(i >= n, i - n, i)


def sigmoid(u):
    return 1.0 / (1.0 + jnp.exp(-u))


class Place:
    def __init__(self, s):
        self.s = s
        self.tm = tm = lax.axis_index("tm")
        self.z = z = lax.axis_index("height")
        self.core = core = tm % 2
        self.yx = yx = tm // 2
        self.x = yx % s.nx
        self.y = yx // s.nx
        self.mate_tm = mate_tm = tm + 1 - 2 * core
        self.z_ring = z_ring = [z] + [wrap(z + d, s.nz) for d in range(1, s.nz)]
        self.x_ring = [self.x] + [wrap(self.x + d, s.nx) for d in range(1, s.nx)]
        self.y_ring = [self.y] + [wrap(self.y + d, s.ny) for d in range(1, s.ny)]
        self.rings = {"y": self.y_ring, "x": self.x_ring}
        self.row = [self.tm_of(self.y, q, core) for q in self.x_ring]
        self.column = [self.tm_of(q, self.x, core) for q in self.y_ring]
        self.lines = {"y": self.column, "x": self.row}
        self.groups = (
            (core * s.nz + z, [(tm, q) for q in z_ring[1:]] + [(mate_tm, q) for q in z_ring]),
            (yx, [(wrap(yx + d, s.nyx) * 2 + core, z) for d in range(1, s.nyx)]),
        )
        self.tm_next, self.tm_prev = wrap(tm + 1, s.tm), wrap(tm + s.tm - 1, s.tm)
        self.z_next, self.z_prev = z_ring[1], z_ring[-1]
        self.partners = [peer for _, peers in self.groups for peer in peers]
        self.partners = self.partners + [
            (t, q) for t in (self.tm_next, self.tm_prev) for q in (z, self.z_next, self.z_prev)
        ]
        self.partners = self.partners + [
            (t, q) for line in (self.row, self.column) for t in line[1:] for q in z_ring[1:]
        ]

    def tm_of(self, y, x, core):
        return (y * self.s.nx + x) * 2 + core

    def greet(self):
        barrier = pltpu.get_barrier_semaphore()
        for partner in self.partners:
            pl.semaphore_signal(barrier, inc=1, device_id=partner, device_id_type=MESH)

    def meet(self):
        pl.semaphore_wait(pltpu.get_barrier_semaphore(), len(self.partners))

    def own_block(self, ref, lo):
        return ref.at[pl.ds(lo, self.s.frames), pl.ds(1, self.s.rows)]

    def own(self, ref):
        return ref[...].astype(F32).reshape(-1, C)

    def bind(self, ar, ar_send, ar_recv, halo_send, halo_recv):
        self.ar, self.ar_send, self.ar_recv = ar, ar_send, ar_recv
        self.halo_send, self.halo_recv = halo_send, halo_recv

    def ar_start(self, k, stage, payload):
        i = 2 * k + stage
        slot, peers = self.groups[stage]
        self.ar[i, slot, 0:1] = payload[0]
        self.ar[i, slot, 1:2] = payload[1]
        for peer in peers:
            pltpu.make_async_remote_copy(
                src_ref=self.ar.at[i, slot],
                dst_ref=self.ar.at[i, slot],
                send_sem=self.ar_send.at[i],
                recv_sem=self.ar_recv.at[i],
                device_id=peer,
                device_id_type=MESH,
            ).start()

    def ar_wait(self, k, stage):
        i = 2 * k + stage
        n = self.s.stages[stage]
        bundle(self.ar_recv.at[i], self.ar.at[i, pl.ds(0, n - 1)])
        parts = [self.ar[i, j] for j in range(n)]
        return [p[0:1] for p in parts], [p[1:2] for p in parts]

    def ar_sent(self, k):
        for stage, n in enumerate(self.s.stages):
            i = 2 * k + stage
            bundle(self.ar_send.at[i], self.ar.at[i, pl.ds(0, n - 1)])

    def local_count(self):
        return float(self.s.frames * self.s.rows * self.s.columns * MEMBERS)

    def local_stats(self, v):
        centre = group_total(jnp.sum(v, axis=0, keepdims=True)) / self.local_count()
        spread = group_total(jnp.sum((v - centre) ** 2, axis=0, keepdims=True))
        return centre, spread

    def join_stats(self, parts, count):
        means, spreads = parts
        centre = sum(means) / float(len(means))
        spread = sum(spreads) + count * sum((mean - centre) ** 2 for mean in means)
        return centre, spread

    def stats_stage(self, k, stage):
        count = self.local_count()
        for n in self.s.stages[:stage]:
            count = count * n
        joined = self.join_stats(self.ar_wait(k, stage), count)
        if stage < 1:
            return self.ar_start(k, stage + 1, joined)
        centre, spread = joined
        return centre, lax.rsqrt(spread / (count * self.s.stages[stage]) + EPSILON)

    def sums_stage(self, k, stage):
        first, second = self.ar_wait(k, stage)
        totals = sum(first), sum(second)
        return totals if stage == 1 else self.ar_start(k, stage + 1, totals)

    def halo_start(self, q, ref, ahead):
        F, R, z = self.s.frames, self.s.rows, self.z
        target = self.tm_next if ahead else self.tm_prev
        far, near = (0, 2) if ahead else (2, 0)
        frames = pl.ds(near, F)
        everything = ref.at[frames, pl.ds(1, R)]
        top, bottom = ref.at[frames, pl.ds(1, 1)], ref.at[frames, pl.ds(R, 1)]
        copies = [
            (everything, ref.at[pl.ds(far, F), pl.ds(1, R)], (target, z)),
            (top, ref.at[pl.ds(near, F), pl.ds(R + 1, 1)], (self.tm, self.z_prev)),
            (bottom, ref.at[pl.ds(near, F), pl.ds(0, 1)], (self.tm, self.z_next)),
            (top, ref.at[pl.ds(far, F), pl.ds(R + 1, 1)], (target, self.z_prev)),
            (bottom, ref.at[pl.ds(far, F), pl.ds(0, 1)], (target, self.z_next)),
        ]
        for piece, place, device in copies:
            pltpu.make_async_remote_copy(
                src_ref=piece,
                dst_ref=place,
                send_sem=self.halo_send.at[q],
                recv_sem=self.halo_recv.at[q],
                device_id=device,
                device_id_type=MESH,
            ).start()

    def halo_bytes(self, sem, ref):
        F, R = self.s.frames, self.s.rows
        bundle(sem, ref.at[pl.ds(0, F + 2), pl.ds(0, F * (R + 4) // (F + 2))])

    def halo_wait(self, q, ref):
        self.halo_bytes(self.halo_recv.at[q], ref)

    def halo_sent(self, q, ref):
        self.halo_bytes(self.halo_send.at[q], ref)


def blank_next(place, ref):
    F = place.s.frames

    @pl.when(place.tm == place.s.tm - 1)
    def _():
        ref[F : F + 2] = jnp.zeros((2,) + ref.shape[1:], ref.dtype)


def copy_first(place, ref):
    @pl.when(place.tm == 0)
    def _():
        ref[0] = ref[2]
        ref[1] = ref[2]


def kernel(
    s,
    x_hbm,
    u_hbm,
    w1_hbm,
    w2_hbm,
    g1_hbm,
    s1_hbm,
    g2_hbm,
    s2_hbm,
    out_hbm,
    ig_hbm,
    wo1_hbm,
    wo2_hbm,
    gg1_hbm,
    sg1_hbm,
    gg2_hbm,
    sg2_hbm,
    w1_ref,
    w2_ref,
    wf1,
    wf2,
    vectors,
    out_ref,
    ig_ref,
    wo,
    results,
    xe,
    ue,
    he,
    ge,
    a1,
    a2,
    g3,
    dact,
    pre_buf,
    ar,
    wg,
    r1,
    p1,
    rx,
    arrivals,
    ar_send,
    ar_recv,
    halo_send,
    halo_recv,
    w_send,
    w_recv,
    load_sem,
    store_sem,
):
    F, R, W = s.frames, s.rows, s.columns
    E, RE = F + 2, R + 2
    cells = R * W
    place = Place(s)
    place.bind(ar, ar_send, ar_recv, halo_send, halo_recv)
    tm, z, x, y, core = place.tm, place.z, place.x, place.y, place.core
    mate_tm, z_ring = place.mate_tm, place.z_ring

    x_ref, u_ref = place.own_block(xe, 2), place.own_block(ue, 0)
    loads = [
        (x_hbm, x_ref),
        (u_hbm, u_ref),
        (w1_hbm, w1_ref),
        (w2_hbm, w2_ref),
        (g1_hbm, vectors.at[0]),
        (s1_hbm, vectors.at[1]),
        (g2_hbm, vectors.at[2]),
        (s2_hbm, vectors.at[3]),
    ]
    loads = [pltpu.make_async_copy(a, b, load_sem.at[i]) for i, (a, b) in enumerate(loads)]
    for load in loads:
        load.start()
    place.greet()

    def shifted(v, dst, f):
        column = lax.broadcasted_iota(jnp.int32, v.shape, 0) & (W - 1)
        left = jnp.where(column == 0, 0.0, pltpu.roll(v, 1, 0))
        right = jnp.where(column == W - 1, 0.0, pltpu.roll(v, RE * W - 1, 0))
        for k, piece in enumerate((left, v, right)):
            dst[f, :, :, k * C : (k + 1) * C] = piece.astype(BF16).reshape(RE, W, C)

    def blank_rows(dst):
        blank = jnp.zeros((E, 1) + dst.shape[2:], dst.dtype)

        @pl.when(z == 0)
        def _():
            dst[:, 0:1] = blank

        @pl.when(z == s.nz - 1)
        def _():
            dst[:, R + 1 : R + 2] = blank

    def build_act(src, dst, stats, gain, shift):
        centre, inverse = stats
        scale = inverse * gain

        def frame(f, carry):
            v = src[f].astype(F32).reshape(RE * W, C)
            affine = (v - centre) * scale + shift
            shifted(affine * sigmoid(affine), dst, f)
            return carry

        lax.fori_loop(0, E, frame, 0)
        blank_rows(dst)

    def build_grad(src):
        def frame(f, carry):
            shifted(src[f].astype(F32).reshape(RE * W, C), g3, f)
            return carry

        lax.fori_loop(0, E, frame, 0)
        blank_rows(g3)

    def dot(a, b):
        return jnp.dot(a, b, preferred_element_type=F32)

    def turn(src, dst):
        for at in range(27):
            dst[at // 9, (at % 9) * C : (at % 9 + 1) * C, :] = src[26 - at].T

    def patches(src, f):
        return jnp.concatenate([src[f, j : j + R].reshape(cells, 3 * C) for j in range(3)], axis=1)

    def conv(src, taps):
        first = dot(patches(src, 0), taps[0])
        second = None
        for f in (1, 2):
            both = dot(patches(src, f), jnp.concatenate([taps[f], taps[f - 1]], axis=1))
            first = first + both[:, :C]
            second = both[:, C:] if second is None else second + both[:, C:]
        return first, second + dot(patches(src, 3), taps[2])

    def taps_of(weight):
        return [weight[9 * i : 9 * i + 9].reshape(9 * C, C) for i in range(3)]

    def back_conv(src, weight):
        dact[0], dact[1] = conv(src, [weight[i] for i in range(3)])

    def back_first(src, weight):
        @pl.when(tm == 0)
        def _():
            both = dot(patches(src, 0), jnp.concatenate([weight[1], weight[2]], axis=1))
            dact[0] += both[:, :C] + both[:, C:] + dot(patches(src, 1), weight[2])

    def weight_grad(act, grad, q):
        turned = [grad[f].reshape(cells, C).T for f in range(F)]
        both = jnp.concatenate(turned, axis=0)
        wg[q, 14 * C : 15 * C, :] = jnp.zeros((C, C), BF16)
        mate = (mate_tm, z)

        def row_tap(j, base):
            window = [act[f, pl.ds(j, R)].reshape(cells, 3 * C) for f in range(E)]
            one, two = dot(both, window[1]), dot(both, window[2])
            sums = (
                dot(turned[0], window[0]) + one[C:],
                one[:C] + two[C:],
                two[:C] + dot(turned[1], window[3]),
            )
            for i, total in enumerate(sums):
                total = total.astype(BF16)
                for k in range(3):
                    at = 3 * i + k
                    lo = base(at) * C
                    wg[q, pl.ds(pl.multiple_of(lo, C), C), :] = total[:, k * C : (k + 1) * C]

        def send(i, src, dst, taps):
            pltpu.make_async_remote_copy(
                src_ref=wg.at[q, pl.ds(pl.multiple_of(src * C, C), taps * C)],
                dst_ref=r1.at[q, pl.ds(pl.multiple_of(dst * C, C), taps * C)],
                send_sem=w_send.at[q, i],
                recv_sem=w_recv.at[q, i],
                device_id=mate,
                device_id_type=MESH,
            ).start()

        row_tap(2 - 2 * core, lambda at: (1 - core) * 19 + at)
        send(0, (1 - core) * 19, (1 - core) * 5, 9)
        row_tap(1, lambda at: 9 + at if at < 5 else 10 + at)
        send(1, 14 - core * 5, core * 9, 5)
        row_tap(2 * core, lambda at: core * 19 + at)

    def norm_back_sums(values, stats, gain, shift):
        centre, inverse = stats
        total_cross = jnp.zeros((1, C), F32)
        total = jnp.zeros((1, C), F32)
        for f in range(F):
            normed = (values[f].astype(F32).reshape(cells, C) - centre) * inverse
            affine = normed * gain + shift
            sig = sigmoid(affine)
            pre = dact[f] * sig * (1.0 + affine * (1.0 - sig))
            pre_buf[f] = pre
            total_cross += jnp.sum(pre * normed, axis=0, keepdims=True)
            total += jnp.sum(pre, axis=0, keepdims=True)
        return total_cross, total

    def norm_back_value(values, stats, gain, sums, f):
        centre, inverse = stats
        gain_grad, shift_grad = sums
        members = float(F * cells * MEMBERS * s.tm * s.nz)
        mean_grad = group_total(gain * shift_grad) / members
        mean_cross = group_total(gain * gain_grad) / members
        normed = (values[f].astype(F32).reshape(cells, C) - centre) * inverse
        return inverse * (pre_buf[f] * gain - mean_grad - normed * mean_cross)

    def weight_sum(q, home, arrivals, relay):
        out = wo.at[q]
        mate = (mate_tm, z)
        mine = core * s.half
        spot = {"y": y, "x": x}
        parts = []
        lo = at = 0
        for p, (first, second, rows, z_lo, z_count) in enumerate(s.parts[q]):
            part = types.SimpleNamespace(p=p, first=first, second=second, lo=lo, at=at, z_lo=z_lo)
            part.zs = range(z_lo, z_lo + z_count)
            part.n = s.size[first]
            part.one = rows // part.n
            part.tile = part.one // (s.size[second] * z_count)
            part.ring, part.line = place.rings[first], place.lines[first]
            part.owner = jnp.logical_and(z >= z_lo, z < z_lo + z_count)
            part.slot = z * s.size[second] + spot[second]
            part.own = ((z - z_lo) * s.size[second] + spot[second]) * part.tile
            lo, at = lo + rows, at + part.one
            parts.append(part)
        plane = s.nz * 4

        def span(lo, rows):
            return pl.ds(pl.multiple_of(lo, 16), rows)

        def send(i, src, dst, device, arrival=None):
            pltpu.make_async_remote_copy(
                src_ref=src,
                dst_ref=dst,
                send_sem=w_send.at[q, i],
                recv_sem=w_recv.at[q, i if arrival is None else arrival],
                device_id=device,
                device_id_type=MESH,
            ).start()

        def arrived(i, rows):
            bundle(w_recv.at[q, i], wg.at[q, pl.ds(0, rows)])

        def sent(i, rows):
            bundle(w_send.at[q, i], wg.at[q, pl.ds(0, rows)])

        def add_mate(part):
            def piece(t, carry):
                rows = span(t * C, C)
                kept = wg[q, span(mine + t * C, C)].astype(F32)
                p1[q, rows] = (kept + r1[q, rows].astype(F32)).astype(BF16)
                return carry

            lax.fori_loop(part.lo // C, (part.lo + part.n * part.one) // C, piece, 0)

        def rows_of(part, i, skip=0, rows=None):
            return span(part.lo + i * part.one + skip, part.one if rows is None else rows)

        def step_mate():
            arrived(0, 9 * C)
            arrived(1, 5 * C)
            for part in parts:
                add_mate(part)
                if relay:
                    half = part.one // 2
                    far = part.ring[2]
                    one = p1.at[q, rows_of(part, far, 0, half)]
                    two = p1.at[q, rows_of(part, far, half, half)]
                    send(2, one, arrivals[0].at[0], (part.line[1], z))
                    send(2, two, arrivals[0].at[1], (part.line[3], z))
                else:
                    for d in range(1, part.n):
                        src = p1.at[q, rows_of(part, part.ring[d])]
                        dst = arrivals[part.p].at[part.ring[0]]
                        send(2 + part.p, src, dst, (part.line[d], z))

        def step_relay():
            (part,) = parts
            half = part.one // 2
            arrived(2, part.one)
            for side, to, skip in ((0, 1, 0), (1, 3, half)):
                rows = rows_of(part, part.ring[to], skip, half)
                total = p1[q, rows].astype(F32) + arrivals[0][side].astype(F32)
                p1[q, rows] = total.astype(BF16)
            for side, to in ((0, 1), (1, 3)):
                src = p1.at[q, rows_of(part, part.ring[to])]
                send(3, src, arrivals[1].at[side], (part.line[to], z))

        def step_plane():
            for part in parts:
                total = p1[q, rows_of(part, part.ring[0])].astype(F32)
                if relay:
                    arrived(3, 2 * part.one)
                    total += arrivals[1][0].astype(F32) + arrivals[1][1].astype(F32)
                else:
                    arrived(2 + part.p, (part.n - 1) * part.one)
                    for d in range(1, part.n):
                        total += arrivals[part.p][part.ring[d]].astype(F32)
                r1[q, part.at : part.at + part.one] = total.astype(BF16)
                across, line = place.rings[part.second], place.lines[part.second]
                for d in range(s.size[part.second]):
                    for owner_z in part.zs:

                        def go(part=part, d=d, owner_z=owner_z, across=across, line=line):
                            tile = (owner_z - part.z_lo) * s.size[part.second] + across[d]
                            src = r1.at[q, span(part.at + tile * part.tile, part.tile)]
                            dst = rx.at[q, part.slot, pl.ds(0, part.tile)]
                            send(4 + part.p, src, dst, (line[d], owner_z), 4)

                        if d:
                            go()
                        else:
                            pl.when(z != owner_z)(go)

        def step_own():
            for part in parts:

                @pl.when(part.owner)
                def _(part=part):
                    arrived(4, (plane - 1) * part.tile)
                    tile = pl.ds(0, part.tile)
                    rx[q, part.slot, tile] = r1[q, span(part.at + part.own, part.tile)]
                    total = rx[q, 0, tile].astype(F32)
                    for j in range(1, plane):
                        total += rx[q, j, tile].astype(F32)
                    lo = mine + part.lo + part.ring[0] * part.one + part.own
                    rows = span(lo, part.tile)
                    out[rows] = total.astype(BF16)
                    for t, column in enumerate(place.lines[part.second]):
                        for d, other in enumerate(z_ring):
                            if t or d:
                                send(6 + part.p, out.at[rows], out.at[rows], (column, other))

        def chunk(part, i, skip=0, rows=None):
            return span(mine + part.lo + i * part.one + skip, part.one if rows is None else rows)

        def step_ring():
            for part in parts:

                @pl.when(part.owner)
                def _(part=part):
                    arrived(6 + part.p, part.one - part.tile)

                @pl.when(jnp.logical_not(part.owner))
                def _(part=part):
                    arrived(6 + part.p, part.one)

                rows = chunk(part, part.ring[0])
                for d in (1, 3) if relay else range(1, part.n):
                    send(8 + part.p, out.at[rows], out.at[rows], (part.line[d], z))

        def step_relay_back():
            (part,) = parts
            half = part.one // 2
            arrived(8, 2 * part.one)
            rows = chunk(part, part.ring[3], 0, half)
            send(9, out.at[rows], out.at[rows], (part.line[1], z))
            rows = chunk(part, part.ring[1], half, half)
            send(9, out.at[rows], out.at[rows], (part.line[3], z))

        def keep():
            return pltpu.make_async_copy(
                out.at[span(mine, s.half)], home.at[span(mine, s.half)], store_sem.at[6 + q]
            )

        def step_deliver():
            for part in parts:
                if relay:
                    arrived(9, part.one)
                else:
                    arrived(8 + part.p, (part.n - 1) * part.one)
                rows = span(mine + part.lo, part.n * part.one)
                send(16, out.at[rows], home.at[rows], mate)
            keep().start()

        def step_end():
            arrived(16, s.half)
            keep().wait()

        def finish():
            sent(0, 9 * C)
            sent(1, 5 * C)
            sent(16, s.half)
            for part in parts:
                if relay:
                    sent(2, part.one)
                    sent(3, 2 * part.one)
                    sent(8, 2 * part.one)
                    sent(9, part.one)
                else:
                    sent(2 + part.p, (part.n - 1) * part.one)
                    sent(8 + part.p, (part.n - 1) * part.one)

                @pl.when(part.owner)
                def _(part=part):
                    sent(4 + part.p, part.one - part.tile)
                    sent(6 + part.p, (plane - 1) * part.tile)

                @pl.when(jnp.logical_not(part.owner))
                def _(part=part):
                    sent(4 + part.p, part.one)

        if relay:
            steps = [step_mate, step_relay, step_plane, step_own, step_ring, step_relay_back]
        else:
            steps = [step_mate, step_plane, step_own, step_ring]
        return steps + [step_deliver, step_end, finish]

    def store(i, src, dst):
        copy = pltpu.make_async_copy(src, dst, store_sem.at[i])
        copy.start()
        return copy

    loads[0].wait()
    payload = place.local_stats(place.own(x_ref))
    place.meet()
    place.ar_start(0, 0, payload)
    place.halo_start(0, xe, True)
    loads[1].wait()
    place.halo_start(1, ue, False)
    for load in loads[2:]:
        load.wait()
    gain1, shift1, gain2, shift2 = (vectors[i] for i in range(4))
    turn(w2_ref, wf2)
    place.stats_stage(0, 0)
    turn(w1_ref, wf1)
    place.halo_wait(0, xe)
    copy_first(place, xe)
    stats1 = place.stats_stage(0, 1)

    build_act(xe, a1, stats1, gain1, shift1)
    for f, value in enumerate(conv(a1, taps_of(w1_ref))):
        he[2 + f, 1 : R + 1] = value.astype(BF16).reshape(R, W, C)
    hidden = place.own_block(he, 2)
    place.ar_start(1, 0, place.local_stats(place.own(hidden)))
    place.halo_wait(1, ue)
    blank_next(place, ue)
    build_grad(ue)
    place.stats_stage(1, 0)
    place.halo_start(2, he, True)
    back_conv(g3, wf2)
    back_first(g3, wf2)
    place.halo_wait(2, he)
    copy_first(place, he)
    stats2 = place.stats_stage(1, 1)

    second = iter(weight_sum(1, wo2_hbm, arrivals[2:], True))
    first = iter(weight_sum(0, wo1_hbm, arrivals[:2], False))
    place.ar_start(2, 0, norm_back_sums(hidden, stats2, gain2, shift2))
    build_act(he, a2, stats2, gain2, shift2)
    place.sums_stage(2, 0)
    weight_grad(a2, u_ref, 1)
    sums2 = place.sums_stage(2, 1)
    for f in range(F):
        value = norm_back_value(hidden, stats2, gain2, sums2, f)
        ge[f, 1 : R + 1] = value.astype(BF16).reshape(R, W, C)
    place.halo_start(3, ge, False)
    next(second)()
    weight_grad(a1, place.own_block(ge, 0), 0)
    next(second)()
    next(first)()
    place.halo_wait(3, ge)
    blank_next(place, ge)
    build_grad(ge)
    back_conv(g3, wf1)
    back_first(g3, wf1)
    place.ar_start(3, 0, norm_back_sums(x_ref, stats1, gain1, shift1))
    next(second)()
    next(first)()
    branch = conv(a2, taps_of(w2_ref))
    for f in range(F):
        total = x_ref[f].astype(F32).reshape(cells, C) + branch[f]
        out_ref[f] = total.astype(BF16).reshape(R, W, C)
    stores = [store(0, out_ref, out_hbm)]
    place.sums_stage(3, 0)
    next(second)()
    next(first)()
    next(second)()
    sums1 = place.sums_stage(3, 1)
    for f in range(F):
        value = norm_back_value(x_ref, stats1, gain1, sums1, f)
        total = u_ref[f].astype(F32).reshape(cells, C) + value
        ig_ref[f] = total.astype(BF16).reshape(R, W, C)
    stores.append(store(1, ig_ref, ig_hbm))
    for i, (row, result) in enumerate(zip(sums1 + sums2, (gg1_hbm, sg1_hbm, gg2_hbm, sg2_hbm))):
        results[i] = row
        stores.append(store(2 + i, results.at[i], result))
    next(first)()
    next(second)()
    next(first)()
    next(second)()
    next(first)()
    next(second)()

    for copy in stores:
        copy.wait()
    next(second)()
    next(first)()
    for k in range(4):
        place.ar_sent(k)
    for q, ref in enumerate((xe, ue, he, ge)):
        place.halo_sent(q, ref)


def finish_kernel(*refs):
    sources, places, (fields, vectors, narrow, wide, load_sem, sem) = refs[:8], refs[8:16], refs[16:]
    copies = []

    def load(i, src, dst):
        copy = pltpu.make_async_copy(src, dst, load_sem.at[i])
        copy.start()
        return copy

    def write(src, dst):
        copy = pltpu.make_async_copy(src, dst, sem.at[len(copies)])
        copy.start()
        copies.append(copy)

    spans = ((0, 9), (9, 10), (19, 9))
    weights = []
    for j, (lo, count) in enumerate(spans):
        for q in range(2):
            rows = pl.ds(lo * C, count * C)
            weights.append(load(2 * j + q, sources[2 + q].at[rows], narrow.at[q, rows]))
    bounce = [(i, fields.at[i]) for i in range(2)] + [(4 + i, vectors.at[i]) for i in range(4)]
    others = [load(6 + n, sources[i], ref) for n, (i, ref) in enumerate(bounce)]
    for j, (lo, count) in enumerate(spans):
        for q in range(2):
            weights[2 * j + q].wait()
            for i in range(3):
                to = (9 * i + 3 * j) * C
                for k in range(3):
                    at = 3 * i + k
                    tap = lo + at + (1 if count == 10 and at >= 5 else 0)
                    block = narrow[q, tap * C : (tap + 1) * C]
                    wide[q, to + k * C : to + (k + 1) * C] = block.T.astype(F32)
                rows = pl.ds(to, 3 * C)
                write(wide.at[q, rows], places[2 + q].at[rows])
        if j == 0:
            for copy, (i, ref) in zip(others, bounce):
                copy.wait()
                write(ref, places[i])
    for copy in copies:
        copy.wait()


def body(inputs, gain1, shift1, weight1, gain2, shift2, weight2, upstream):
    F, R, W, _ = inputs.shape
    s = plan_of(lax.axis_size("tm"), lax.axis_size("height"), F, R, W)
    E, RE = F + 2, R + 2
    cells = R * W
    hbm = pl.BlockSpec(memory_space=pltpu.HBM)
    field = jax.ShapeDtypeStruct(inputs.shape, BF16)
    weights = jax.ShapeDtypeStruct((s.taps * C, C), BF16)
    vector = jax.ShapeDtypeStruct((1, C), F32)
    wide = pltpu.VMEM((E, RE, W, C), BF16)
    wider = pltpu.VMEM((E, RE, W, 3 * C), BF16)
    arrivals = []
    for first, _, rows, _, _ in s.parts[0]:
        arrivals.append(pltpu.VMEM((s.size[first], rows // s.size[first], C), BF16))
    ((first, _, rows, _, _),) = s.parts[1]
    arrivals.append(pltpu.VMEM((2, rows // s.size[first] // 2, C), BF16))
    arrivals.append(pltpu.VMEM((2, rows // s.size[first], C), BF16))
    room = 60 * 1024 * 1024
    results = pl.pallas_call(
        functools.partial(kernel, s),
        out_shape=[field, field, weights, weights, vector, vector, vector, vector],
        in_specs=[hbm] * 8,
        out_specs=[hbm] * 8,
        scratch_shapes=[
            pltpu.VMEM((27, C, C), BF16),
            pltpu.VMEM((27, C, C), BF16),
            pltpu.VMEM((3, 9 * C, C), BF16),
            pltpu.VMEM((3, 9 * C, C), BF16),
            pltpu.VMEM((4, 1, C), F32),
            pltpu.VMEM((F, R, W, C), BF16),
            pltpu.VMEM((F, R, W, C), BF16),
            pltpu.VMEM((2, s.taps * C, C), BF16),
            pltpu.VMEM((4, 1, C), F32),
            wide,
            wide,
            wide,
            wide,
            wider,
            wider,
            wider,
            pltpu.VMEM((F, cells, C), F32),
            pltpu.VMEM((F, cells, C), F32),
            pltpu.VMEM((8, max(s.stages), 2, C), F32),
            pltpu.VMEM((2, s.taps * C, C), BF16),
            pltpu.VMEM((2, s.half, C), BF16),
            pltpu.VMEM((2, s.half, C), BF16),
            pltpu.VMEM((2, 4 * s.nz, s.tile, C), BF16),
            arrivals,
            pltpu.SemaphoreType.DMA((8,)),
            pltpu.SemaphoreType.DMA((8,)),
            pltpu.SemaphoreType.DMA((4,)),
            pltpu.SemaphoreType.DMA((4,)),
            pltpu.SemaphoreType.DMA((2, 17)),
            pltpu.SemaphoreType.DMA((2, 17)),
            pltpu.SemaphoreType.DMA((8,)),
            pltpu.SemaphoreType.DMA((8,)),
        ],
        compiler_params=pltpu.CompilerParams(
            collective_id=0, has_side_effects=True, vmem_limit_bytes=room
        ),
        cost_estimate=pl.CostEstimate(
            flops=6 * 2 * F * cells * 27 * C * C, bytes_accessed=8_000_000, transcendentals=1_000_000
        ),
    )(
        inputs,
        upstream,
        weight1.reshape(27, C, C),
        weight2.reshape(27, C, C),
        gain1.reshape(1, C),
        shift1.reshape(1, C),
        gain2.reshape(1, C),
        shift2.reshape(1, C),
    )
    total = jax.ShapeDtypeStruct((27 * C, C), F32)
    output, input_grad, first, second, gg1, sg1, gg2, sg2 = pl.pallas_call(
        finish_kernel,
        out_shape=[field, field, total, total, vector, vector, vector, vector],
        in_specs=[hbm] * 8,
        out_specs=[hbm] * 8,
        scratch_shapes=[
            pltpu.VMEM((2, F, R, W, C), BF16),
            pltpu.VMEM((4, 1, C), F32),
            pltpu.VMEM((2, s.taps * C, C), BF16),
            pltpu.VMEM((2, 27 * C, C), F32),
            pltpu.SemaphoreType.DMA((12,)),
            pltpu.SemaphoreType.DMA((24,)),
        ],
        compiler_params=pltpu.CompilerParams(vmem_limit_bytes=room),
        cost_estimate=pl.CostEstimate(flops=0, bytes_accessed=6_000_000, transcendentals=0),
    )(*results)
    return (
        output,
        input_grad,
        first.reshape(3, 3, 3, C, C),
        second.reshape(3, 3, 3, C, C),
        gg1.reshape(C),
        sg1.reshape(C),
        gg2.reshape(C),
        sg2.reshape(C),
    )


def solution(mesh):
    fields = P("tm", "height", None, None)
    return jax.shard_map(
        body,
        mesh=mesh,
        in_specs=(fields, P(), P(), P(), P(), P(), P(), fields),
        out_specs=(fields, fields, P(), P(), P(), P(), P(), P()),
        check_vma=False,
    )
```
